128 devices in a mesh: block: 16 (over z_hi, x, core), tm: 8 (over y, z_lo).
Axes of the slice: x: 4, y: 4, z: 4 (z_hi: 2, z_lo: 2; z = z_hi * 2 + z_lo), core: 2. Of those that a mesh axis runs over, the one named last changes fastest.
Arguments:
- traces: bfloat16 [4096, 16, 6, 1024], P('block', 'tm')
- valid: int32 [4096, 16, 6], P('block', 'tm'), may hold values from 0 to 1, as said below
- panel_owner: int32 [4], replicated, may hold values from 0 to 15, as said below
- panel_start: int32 [4], replicated, may hold values from 0 to 252, as said below
Outputs:
- xcorr: float32 [16, 4096, 1024], P('tm', 'block')
The draws below stay inside these ranges and needn't reach their ends.
Inputs may be any that keep to these rules, and one draw needn't show every extreme that they name: Within one block-tm cell (256 channels by 2 windows by 6 segments) at least an eighth of the segments are valid. `panel_owner`: the panels lie on distinct blocks. `panel_start`: multiples of 4.
All inputs are finite; a program needn't handle non-finite values.
Results may differ from the reference program's by a relative error of at most 0.0051.
Values may be sent and summed in bfloat16 or wider, within the bound.
A program may use at most 128 MiB of HBM per device.

```python
import math
import jax
import jax.numpy as jnp
from jax import lax

CB = 256
C = 4096
WD = 2
WINDOWS = 16
S = 6
L = 1024
F = 512
PP = 4
NP = 4
P_SIZE = 16
SEGS_DEV = 3072
CAP = 1536


def draw_traces(key, part):
    noise_key, shared_key, scale_key = jax.random.split(key, 3)
    noise_part = jax.random.normal(noise_key, (C, WINDOWS, S, L), jnp.float32)
    shared_weight = 0.15
    lowest = 0.2
    highest = 5.0
    shared = jax.random.normal(shared_key, (WINDOWS, S, L), jnp.float32)
    row_scale = jnp.exp(jax.random.uniform(scale_key, (C, WINDOWS, S, 1), jnp.float32, math.log(lowest), math.log(highest)))
    return (row_scale * (noise_part + shared_weight * shared[None])).astype(jnp.bfloat16)


def draw_valid(key, part):
    block_count = C // CB
    time_count = WINDOWS // WD
    cell_count = block_count * time_count
    count_key, chosen_key, perm_key = jax.random.split(jax.random.fold_in(key, 11), 3)
    counts = jax.random.randint(count_key, (cell_count,), SEGS_DEV // 8, CAP + 1)
    chosen = jax.random.randint(chosen_key, (), 0, cell_count)
    counts = jnp.where(jnp.arange(cell_count) == chosen, CAP, counts)
    cell_keys = jax.random.split(perm_key, cell_count)
    ranked = jax.vmap(lambda cell_key: jax.random.permutation(cell_key, SEGS_DEV))(cell_keys)
    marks = (ranked < counts[:, None]).astype(jnp.int32)
    marks = marks.reshape(block_count, time_count, CB, WD, S).transpose(0, 2, 1, 3, 4)
    return marks.reshape(C, WINDOWS, S)


def draw_panel_owner(key, part):
    block_count = C // CB
    middle_key, order_key = jax.random.split(jax.random.fold_in(key, 23), 2)
    middle = (jax.random.permutation(middle_key, block_count - 2)[:NP - 2] + 1).astype(jnp.int32)
    joined = jnp.concatenate([jnp.zeros((1,), jnp.int32), middle, jnp.full((1,), block_count - 1, jnp.int32)])
    return jax.random.permutation(order_key, joined).astype(jnp.int32)


def draw_panel_start(key, part):
    start_key, chosen_key = jax.random.split(jax.random.fold_in(key, 37), 2)
    starts = jax.random.randint(start_key, (NP,), 0, CB // PP).astype(jnp.int32)
    chosen = jax.random.randint(chosen_key, (), 0, NP)
    places = jnp.arange(NP, dtype=jnp.int32)
    starts = jnp.where(places == chosen, CB // PP - 1, starts)
    starts = jnp.where(places == (chosen + 1) % NP, 0, starts)
    return (starts * PP).astype(jnp.int32)


def setup_inputs(seed: int = 0) -> dict:
    key_list = jax.random.split(jax.random.key(seed), 5)
    return {
        "traces": draw_traces(jax.random.fold_in(key_list[4], 71), 0),
        "valid": draw_valid(jax.random.fold_in(key_list[4], 71), 0),
        "panel_owner": draw_panel_owner(jax.random.fold_in(key_list[4], 71), 0),
        "panel_start": draw_panel_start(jax.random.fold_in(key_list[4], 71), 0),
    }


def forward_table(length):
    sample = jnp.arange(length, dtype=jnp.int32)
    bin_index = jnp.arange(length // 2, dtype=jnp.int32)
    angles = (sample[:, None] * bin_index[None, :] % length).astype(jnp.float32) * (2.0 * math.pi / length)
    return jnp.concatenate([jnp.cos(angles), -jnp.sin(angles)], axis=1).astype(jnp.bfloat16)

def inverse_table(length, factor):
    bin_index = jnp.arange(length // 2, dtype=jnp.int32)
    lag_index = jnp.arange(length, dtype=jnp.int32)
    angles = (bin_index[:, None] * lag_index[None, :] % length).astype(jnp.float32) * (2.0 * math.pi / length)
    weight = jnp.where(bin_index == 0, 1.0, 2.0).astype(jnp.float32)[:, None] * factor
    return jnp.concatenate([weight * jnp.cos(angles), -weight * jnp.sin(angles)], axis=0)

def whiten(segment_rows, valid_mask, forward):
    spectrum = jnp.dot(segment_rows, forward, preferred_element_type=jnp.float32)
    energy = lax.optimization_barrier(jnp.mean(spectrum * spectrum, axis=1, keepdims=True))
    return (spectrum * lax.rsqrt(energy + 1e-06) * valid_mask[:, None].astype(jnp.float32)).astype(jnp.bfloat16)

def correlate(left, right):
    bins = left.shape[-1] // 2
    left = left.astype(jnp.float32)
    right = right.astype(jnp.float32)
    left_both = jnp.concatenate([left[..., :bins], left[..., bins:]], axis=1)
    right_both = jnp.concatenate([right[..., :bins], right[..., bins:]], axis=1)
    right_turn = jnp.concatenate([right[..., bins:], -right[..., :bins]], axis=1)
    real_part = jnp.einsum('jmk,imk->jik', left_both, right_both)
    imag_part = jnp.einsum('jmk,imk->jik', left_both, right_turn)
    return jnp.concatenate([real_part, imag_part], axis=-1)

def reference(traces, valid, panel_owner, panel_start):
    forward = forward_table(L)
    inverse = inverse_table(L, 1.0 / math.sqrt(F * WINDOWS * S))
    offsets = jnp.arange(PP, dtype=jnp.int32)
    source = (panel_owner[:, None] * CB + panel_start[:, None] + offsets[None, :]).reshape(P_SIZE).astype(jnp.int32)
    panel_rows = traces[source].reshape(P_SIZE * WINDOWS * S, L)
    panel_mask = valid[source].reshape(P_SIZE * WINDOWS * S)
    sources = whiten(panel_rows, panel_mask, forward).reshape(P_SIZE, WINDOWS * S, 2 * F)

    def one_block(block_args):
        block_traces, block_valid = block_args
        whitened = whiten(block_traces.reshape(CB * WINDOWS * S, L), block_valid.reshape(CB * WINDOWS * S), forward)
        cross_spec = correlate(sources, whitened.reshape(CB, WINDOWS * S, 2 * F))
        return jnp.dot(cross_spec, inverse, precision=lax.Precision.HIGHEST)
    blocks = lax.map(one_block, (traces.reshape(C // CB, CB, WINDOWS, S, L), valid.reshape(C // CB, CB, WINDOWS, S)))
    return blocks.transpose(1, 0, 2, 3).reshape(P_SIZE, C, L)
```

```python
import functools
import math

import jax
import jax.numpy as jnp
import ml_dtypes
import numpy as np
from jax import lax
from jax.experimental import pallas as pl
from jax.experimental.pallas import tpu as pltpu
from jax.sharding import PartitionSpec as P

MESH = pl.DeviceIdType.MESH
PP = 4
NP = 4
J = PP * NP
GB = 8
PAIR = 2 * GB
KB = 32
GP = KB // PAIR
RJ = GP * 2 * PAIR
NZ = 8
NT = (((1,), (1,)), ((), ()))


def forward_t(length):
    k = np.arange(length // 2)
    n = np.arange(length)
    a = (k[:, None] * n[None, :] % length) * (2.0 * math.pi / length)
    return np.concatenate([np.cos(a), -np.sin(a)], axis=0).astype(np.float32).astype(ml_dtypes.bfloat16)


def inverse_rows(length, factor):
    bins = length // 2
    k = np.arange(bins)
    t = np.arange(length)
    a = (k[:, None] * t[None, :] % length) * (2.0 * math.pi / length)
    w = np.where(k == 0, 1.0, 2.0)[:, None] * factor
    full = np.stack([w * np.cos(a), -w * np.sin(a)])
    full = full.reshape(2, bins // PAIR, PAIR, length).transpose(1, 0, 2, 3)
    return full.reshape(length, length).astype(np.float32).astype(ml_dtypes.bfloat16)


def kernel(dims, x_hbm, ft_hbm, slab, onehot, valid, c_out, xv, ftv, w, scale, p, s, xs,
           rsb, rz1, zfl, zfr, zrl, zrr, yfl, yfr, yrl, yrr, zs, rz2,
           x_sem, ft_sem, rs_send, rs_recv, own_sem, ag_send, ag_recv,
           z1_send, z1_recv, zy_send, zfl_recv, zfr_recv, zrl_recv, zrr_recv,
           yy_send, yfl_recv, yfr_recv, yrl_recv, yrr_recv, z2_send, z2_recv):
    nb, nt, m_count, length = dims
    bins = length // 2
    channels = c_out.shape[-1]
    ny = nt // 2
    nr = nb // 2
    b = lax.axis_index("block")
    t = lax.axis_index("tm")
    y = t // 2
    z = t % 2
    right = (b, (y + 1) % ny * 2 + z)
    left = (b, (y + ny - 1) % ny * 2 + z)
    across = (b, y * 2 + 1 - z)
    yr = (y + 1) % ny
    yl = (y + ny - 1) % ny
    yo = (y + 2) % ny

    def remote(src, dst, send, recv, device):
        return pltpu.make_async_remote_copy(
            src_ref=src, dst_ref=dst, send_sem=send, recv_sem=recv,
            device_id=device, device_id_type=MESH,
        )

    pltpu.make_async_copy(ft_hbm, ftv, ft_sem).start()

    def load(m):
        return pltpu.make_async_copy(x_hbm.at[m], xv.at[m], x_sem.at[m])

    def start_load(m, _):
        load(m).start()
        return 0

    lax.fori_loop(0, m_count, start_load, 0)

    barrier = pltpu.get_barrier_semaphore()

    def greet(e, _):
        @pl.when(e != b)
        def _():
            pl.semaphore_signal(barrier, inc=1, device_id=(e, t), device_id_type=MESH)

        return 0

    lax.fori_loop(0, nb, greet, 0)
    for device in (right, left, across):
        pl.semaphore_signal(barrier, inc=1, device_id=device, device_id_type=MESH)
    pl.semaphore_wait(barrier, nb - 1 + 3)

    def rs_copy(r):
        return remote(slab.at[r], rsb.at[b], rs_send.at[r], rs_recv.at[b], (2 * r, t))

    def rs_start(r, _):
        @pl.when(2 * r != b)
        def _():
            rs_copy(r).start()

        return 0

    lax.fori_loop(0, nr, rs_start, 0)
    reducer = b % 2 == 0
    part = b // 2

    @pl.when(reducer)
    def _():
        pltpu.make_async_copy(slab.at[part], rsb.at[b], own_sem).start()

    def transform(m):
        load(m).wait()
        spectrum = lax.dot_general(ftv[...], xv[m], NT, preferred_element_type=jnp.float32)
        w[m] = spectrum
        energy = jnp.sum(spectrum * spectrum, axis=0, keepdims=True) * (1.0 / length)
        scale[m] = lax.rsqrt(energy + 1e-06) * valid[m]

    def transform_step(m, _):
        transform(m)
        return 0

    pltpu.make_async_copy(ft_hbm, ftv, ft_sem).wait()
    early = m_count // 3
    lax.fori_loop(0, early, transform_step, 0)

    rows_s = m_count * J

    def ag_copy(e):
        return remote(
            xs.at[part], xs.at[part], ag_send.at[e], ag_recv.at[part], (e, t)
        )

    @pl.when(reducer)
    def _():
        pltpu.make_async_copy(slab.at[part], rsb.at[b], own_sem).wait()

        def rs_wait(e, _):
            @pl.when(e != b)
            def _():
                remote(slab.at[0], rsb.at[e], rs_send.at[0], rs_recv.at[e], (e, t)).wait_recv()

            return 0

        lax.fori_loop(0, nb, rs_wait, 0)
        picked = jnp.dot(
            onehot[...], rsb[...].reshape(nb * m_count * PP, length // nr),
            preferred_element_type=jnp.float32,
        )
        xs[part] = picked.astype(jnp.bfloat16)

        def ag_start(e, _):
            @pl.when(e != b)
            def _():
                ag_copy(e).start()

            return 0

        lax.fori_loop(0, nb, ag_start, 0)

    lax.fori_loop(early, m_count, transform_step, 0)

    def ag_wait(r, _):
        @pl.when(2 * r != b)
        def _():
            remote(xs.at[r], xs.at[r], ag_send.at[0], ag_recv.at[r], (2 * r, t)).wait_recv()

        return 0

    lax.fori_loop(0, nr, ag_wait, 0)
    source_rows = jnp.concatenate([xs[r] for r in range(nr)], axis=1)
    source_rows = jnp.concatenate(
        [source_rows, jnp.zeros((256 - rows_s, length), jnp.bfloat16)], axis=0
    )
    spectrum = lax.dot_general(ftv[...], source_rows, NT, preferred_element_type=jnp.float32)
    energy = jnp.sum(spectrum * spectrum, axis=0, keepdims=True) * (1.0 / length)
    s[...] = spectrum * lax.rsqrt(energy + 1e-06)

    def iota(shape, axis):
        return lax.broadcasted_iota(jnp.int32, shape, axis)

    def correlate_group(k0):
        copies = (iota((128, 256), 0) // GB == iota((128, 256), 1) % J).astype(jnp.float32)
        copies = copies.astype(jnp.bfloat16)
        segment = iota((128, 256), 0) // GB == iota((128, 256), 1) // J
        diagonal = iota((128, 256), 0) % GB == iota((128, 256), 1) % GB
        stacked = []
        for base in (0, bins):
            tile = s[pl.ds(pl.multiple_of(base + k0, GB), GB), :]
            stacked.append(jnp.where(segment, jnp.concatenate([tile] * 16, axis=0), 0.0))
        stacked = jnp.concatenate(stacked, axis=0).astype(jnp.bfloat16)
        real = lax.dot_general(copies, stacked, NT, preferred_element_type=jnp.float32)
        real = jnp.where(diagonal, real, 0.0)
        imag = jnp.concatenate([-real[:, 128:], real[:, :128]], axis=1)
        left_side = jnp.concatenate([real, imag], axis=0).astype(jnp.bfloat16)
        rows = []
        for base in (0, bins):
            for m in range(m_count):
                tile = w[m, pl.ds(pl.multiple_of(base + k0, GB), GB), :]
                rows.append(tile * scale[m])
            rows.append(jnp.zeros((128 - m_count * GB, channels), jnp.float32))
        right_side = jnp.concatenate(rows, axis=0).astype(jnp.bfloat16)
        return jnp.dot(left_side, right_side, preferred_element_type=jnp.float32)

    def correlate_chunk(c):
        for g in range(GP):
            k0 = c * KB + g * PAIR
            first = correlate_group(k0).reshape(2, J, GB, channels)
            second = correlate_group(k0 + GB).reshape(2, J, GB, channels)
            both = jnp.concatenate([first, second], axis=2).astype(jnp.bfloat16)
            both = both.reshape(2, ny, 2, 2, PAIR, channels)
            for o in range(2):
                p[c, :, :, :, pl.ds((g * 2 + o) * PAIR, PAIR), :] = both[o]

    def z1(n):
        return remote(p.at[n, :, 1 - z], rz1.at[n], z1_send.at[n], z1_recv.at[n], across)

    def ring(parts, n, fl, fr, rl, rr, send, fl_recv, fr_recv, rl_recv, rr_recv):
        def copy(i):
            src, dst, recv, device = (
                lambda: (parts(yo, 0), fl.at[n], fl_recv.at[n], right),
                lambda: (parts(yo, 1), fr.at[n], fr_recv.at[n], left),
                lambda: (parts(yr, 1), rl.at[n, 1], rl_recv.at[n, 1], right),
                lambda: (parts(yl, 0), rr.at[n, 0], rr_recv.at[n, 0], left),
                lambda: (fl.at[n], rl.at[n, 0], rl_recv.at[n, 0], right),
                lambda: (fr.at[n], rr.at[n, 1], rr_recv.at[n, 1], left),
            )[i]()
            return remote(src, dst, send.at[n, i], recv, device)

        return copy

    def add(a, c):
        return (a.astype(jnp.float32) + c.astype(jnp.float32)).astype(jnp.bfloat16)

    def z_ring(n):
        return ring(lambda o, h: rz1.at[n, o, h], n, zfl, zfr, zrl, zrr,
                    zy_send, zfl_recv, zfr_recv, zrl_recv, zrr_recv)

    def y_ring(n):
        return ring(lambda o, h: p.at[NZ + n, o, h], n, yfl, yfr, yrl, yrr,
                    yy_send, yfl_recv, yfr_recv, yrl_recv, yrr_recv)

    def z2(n):
        return remote(zs.at[n], rz2.at[n], z2_send.at[n], z2_recv.at[n], across)

    def slot(n, _):
        @pl.when(n < NZ)
        def _():
            correlate_chunk(n)
            z1(n).start()
            correlate_chunk(NZ + n)
            for i in range(4):
                y_ring(n)(i).start()

        @pl.when((n >= 1) & (n < NZ + 1))
        def _():
            k = n - 1
            copies = y_ring(k)
            copies(0).wait_recv()
            yfl[k] = add(yfl[k], p[NZ + k, yr, 0])
            copies(4).start()
            copies(1).wait_recv()
            yfr[k] = add(yfr[k], p[NZ + k, yl, 1])
            copies(5).start()
            z1(k).wait_recv()
            rz1[k] = add(rz1[k], p[k, :, z])
            for i in range(4):
                z_ring(k)(i).start()

        @pl.when((n >= 2) & (n < NZ + 2))
        def _():
            k = n - 2
            copies = y_ring(k)
            for i in (2, 3, 4, 5):
                copies(i).wait_recv()
            total = (p[NZ + k, y].astype(jnp.float32) + yrl[k].astype(jnp.float32)
                     + yrr[k].astype(jnp.float32))
            zs[k] = jnp.where(z == 0, total[1], total[0]).astype(jnp.bfloat16)
            c_out[:, NZ + k] = jnp.where(z == 0, total[0], total[1])
            z2(k).start()
            copies = z_ring(k)
            copies(0).wait_recv()
            zfl[k] = add(zfl[k], rz1[k, yr, 0])
            copies(4).start()
            copies(1).wait_recv()
            zfr[k] = add(zfr[k], rz1[k, yl, 1])
            copies(5).start()

        @pl.when(n >= 3)
        def _():
            k = n - 3
            copies = z_ring(k)
            for i in (2, 3, 4, 5):
                copies(i).wait_recv()
            c_out[:, k] = (rz1[k, y].astype(jnp.float32) + zrl[k].astype(jnp.float32)
                           + zrr[k].astype(jnp.float32))
            z2(k).wait_recv()
            c_out[:, NZ + k] += rz2[k].astype(jnp.float32)

        return 0

    lax.fori_loop(0, NZ + 3, slot, 0)

    def rs_drain(r, _):
        @pl.when(2 * r != b)
        def _():
            rs_copy(r).wait_send()

        return 0

    lax.fori_loop(0, nr, rs_drain, 0)

    @pl.when(reducer)
    def _():
        def ag_drain(e, _):
            @pl.when(e != b)
            def _():
                ag_copy(e).wait_send()

            return 0

        lax.fori_loop(0, nb, ag_drain, 0)

    def drain(n, _):
        z1(n).wait_send()
        z2(n).wait_send()
        for i in range(6):
            z_ring(n)(i).wait_send()
            y_ring(n)(i).wait_send()
        return 0

    lax.fori_loop(0, NZ, drain, 0)


def on_device(traces, valid, panel_owner, panel_start):
    channels, windows_here, segments, length = traces.shape
    m_count = windows_here * segments
    nb = lax.axis_size("block")
    nt = lax.axis_size("tm")
    nr = nb // 2
    ny = nt // 2
    b = lax.axis_index("block")
    x = traces.transpose(1, 2, 0, 3).reshape(m_count, channels, length)
    mine = panel_owner == b
    start = jnp.sum(jnp.where(mine, panel_start, 0))
    slab = lax.dynamic_slice_in_dim(traces, start, PP, 0)
    slab_valid = lax.dynamic_slice_in_dim(valid, start, PP, 0)
    slab = jnp.where(slab_valid[..., None] != 0, slab, 0).astype(jnp.bfloat16)
    slab = slab.transpose(1, 2, 0, 3).reshape(m_count * PP, nr, length // nr).transpose(1, 0, 2)
    mask = valid.transpose(1, 2, 0).reshape(m_count, 1, channels).astype(jnp.float32)
    row = jnp.arange(m_count * J, dtype=jnp.int32)
    col = jnp.arange(nb * m_count * PP, dtype=jnp.int32)
    owner = jnp.tile(jnp.repeat(panel_owner, PP), m_count)
    onehot = (
        (owner[:, None] == (col // (m_count * PP))[None, :])
        & ((row // J)[:, None] == (col // PP % m_count)[None, :])
        & ((row % PP)[:, None] == (col % PP)[None, :])
    ).astype(jnp.bfloat16)
    forward = jnp.asarray(forward_t(length))
    inverse = jnp.asarray(
        inverse_rows(length, 1.0 / math.sqrt(length // 2 * m_count * nt))
    )
    bf16, f32 = jnp.bfloat16, jnp.float32
    dma = pltpu.SemaphoreType.DMA
    vmem = pl.BlockSpec(memory_space=pltpu.VMEM)
    hbm = pl.BlockSpec(memory_space=pl.ANY)
    chunks = 2 * NZ
    unit = (RJ, channels)
    cross = pl.pallas_call(
        functools.partial(kernel, (nb, nt, m_count, length)),
        out_shape=jax.ShapeDtypeStruct((2, chunks) + unit, f32),
        in_specs=[hbm, hbm, vmem, vmem, vmem],
        out_specs=vmem,
        scratch_shapes=[
            pltpu.VMEM((m_count, channels, length), bf16),
            pltpu.VMEM((length, length), bf16),
            pltpu.VMEM((m_count, length, channels), f32),
            pltpu.VMEM((m_count, 1, channels), f32),
            pltpu.VMEM((chunks, ny, 2, 2) + unit, bf16),
            pltpu.VMEM((length, 256), f32),
            pltpu.VMEM((nr, m_count * J, length // nr), bf16),
            pltpu.VMEM((nb, m_count * PP, length // nr), bf16),
            pltpu.VMEM((NZ, ny, 2) + unit, bf16),
            pltpu.VMEM((NZ,) + unit, bf16),
            pltpu.VMEM((NZ,) + unit, bf16),
            pltpu.VMEM((NZ, 2) + unit, bf16),
            pltpu.VMEM((NZ, 2) + unit, bf16),
            pltpu.VMEM((NZ, 2) + unit, bf16),
            pltpu.VMEM((NZ, 2) + unit, bf16),
            pltpu.VMEM((NZ, 2, 2) + unit, bf16),
            pltpu.VMEM((NZ, 2, 2) + unit, bf16),
            pltpu.VMEM((NZ, 2) + unit, bf16),
            pltpu.VMEM((NZ, 2) + unit, bf16),
            dma((m_count,)), dma, dma((nr,)), dma((nb,)), dma, dma((nb,)), dma((nr,)),
            dma((NZ,)), dma((NZ,)),
            dma((NZ, 6)), dma((NZ,)), dma((NZ,)), dma((NZ, 2)), dma((NZ, 2)),
            dma((NZ, 6)), dma((NZ,)), dma((NZ,)), dma((NZ, 2)), dma((NZ, 2)),
            dma((NZ,)), dma((NZ,)),
        ],
        compiler_params=pltpu.CompilerParams(
            collective_id=0, has_side_effects=True, vmem_limit_bytes=56 * 2**20
        ),
        name="cross",
    )(x, forward, slab, onehot, mask)
    cross = cross.reshape(2, length, channels).astype(bf16)
    return lax.dot_general(
        cross, inverse, (((1,), (0,)), ((), ())), preferred_element_type=f32
    )


def solution(mesh):
    in_specs = (P("block", "tm", None, None), P("block", "tm", None), P(), P())
    out_specs = P("tm", "block", None)
    return jax.shard_map(
        on_device, mesh=mesh, in_specs=in_specs, out_specs=out_specs, check_vma=False
    )
```

```python
import functools
import math

import jax
import jax.numpy as jnp
import ml_dtypes
import numpy as np
from jax import lax
from jax.experimental import pallas as pl
from jax.experimental.pallas import tpu as pltpu
from jax.sharding import PartitionSpec as P

MESH = pl.DeviceIdType.MESH
PP = 4
NP = 4
J = PP * NP
GB = 8
PAIR = 2 * GB
KB = 32
GP = KB // PAIR
RJ = GP * 2 * PAIR
NZ = 7
NY = 9
NT = (((1,), (1,)), ((), ()))


def forward_t(length):
    k = np.arange(length // 2)
    n = np.arange(length)
    a = (k[:, None] * n[None, :] % length) * (2.0 * math.pi / length)
    return np.concatenate([np.cos(a), -np.sin(a)], axis=0).astype(np.float32).astype(ml_dtypes.bfloat16)


def inverse_rows(length, factor):
    bins = length // 2
    k = np.arange(bins)
    t = np.arange(length)
    a = (k[:, None] * t[None, :] % length) * (2.0 * math.pi / length)
    w = np.where(k == 0, 1.0, 2.0)[:, None] * factor
    full = np.stack([w * np.cos(a), -w * np.sin(a)])
    full = full.reshape(2, bins // PAIR, PAIR, length).transpose(1, 0, 2, 3)
    return full.reshape(length, length).astype(np.float32).astype(ml_dtypes.bfloat16)


def kernel(dims, x_hbm, ft_hbm, valid, owner, first, c_out, xv, ftv, w, scale, p, s, slab, xs,
           rsb, keep, rz1, zfl, zfr, zrl, zrr, yfl, yfr, yrl, yrr, zs, rz2,
           x_sem, ft_sem, rs_send, rs_recv, ag_send, fw_send, ag_recv,
           z1_send, z1_recv, zy_send, zfl_recv, zfr_recv, zrl_recv, zrr_recv,
           yy_send, yfl_recv, yfr_recv, yrl_recv, yrr_recv, z2_send, z2_recv):
    nb, nt, segments, length = dims
    m_count = 2 * segments
    bins = length // 2
    channels = c_out.shape[-1]
    ny = nt // 2
    nr = nb // 2
    lanes = length // nr
    b = lax.axis_index("block")
    t = lax.axis_index("tm")
    part = b // 2
    core = b % 2
    y = t // 2
    z = t % 2
    right = (b, (y + 1) % ny * 2 + z)
    left = (b, (y + ny - 1) % ny * 2 + z)
    across = (b, y * 2 + 1 - z)
    sibling = (part * 2 + 1 - core, t)
    yr = (y + 1) % ny
    yl = (y + ny - 1) % ny
    yo = (y + 2) % ny

    def remote(src, dst, send, recv, device):
        return pltpu.make_async_remote_copy(
            src_ref=src, dst_ref=dst, send_sem=send, recv_sem=recv,
            device_id=device, device_id_type=MESH,
        )

    def iota(shape, axis):
        return lax.broadcasted_iota(jnp.int32, shape, axis)

    def loop(count, body, skip=None):
        def step(i, _):
            if skip is None:
                body(i)
            else:
                pl.when(i != skip)(lambda: body(i))
            return 0

        lax.fori_loop(0, count, step, 0)

    def load(g):
        return pltpu.make_async_copy(x_hbm.at[:, g], xv.at[:, g], x_sem.at[g])

    loop(segments, lambda g: load(g).start())
    pltpu.make_async_copy(ft_hbm, ftv, ft_sem).start()

    barrier = pltpu.get_barrier_semaphore()

    def greet(device):
        pl.semaphore_signal(barrier, inc=1, device_id=device, device_id_type=MESH)

    loop(nb, lambda e: greet((e, t)), b)
    for device in (right, left, across):
        greet(device)

    loop(segments, lambda g: load(g).wait())
    start = 0
    for panel in range(NP):
        start = start + jnp.where(owner[panel] == b, first[panel], 0)
    valid_rows = valid[...].reshape(m_count, channels).astype(jnp.float32)
    for q in range(PP):
        good = jnp.sum(
            jnp.where(iota((m_count, channels), 1) == start + q, valid_rows, 0.0),
            axis=1, keepdims=True,
        )
        rows = xv[start + q].reshape(m_count, length).astype(jnp.float32) * good
        rows = jnp.concatenate([rows, jnp.zeros((16 - m_count, length), jnp.float32)], axis=0)
        rows = rows.astype(jnp.bfloat16)
        for r in range(nr):
            slab[r, q // 2, pl.ds(q % 2 * 16, 16), :] = rows[:, r * lanes:(r + 1) * lanes]
    pl.semaphore_wait(barrier, nb - 1 + 3)

    def rs_copy(e):
        return remote(slab.at[e // 2, e % 2], rsb.at[b], rs_send.at[e], rs_recv.at[b], (e, t))

    def rs_arrived(e):
        remote(slab.at[part, core], rsb.at[e], rs_send.at[e], rs_recv.at[e], (e, t)).wait_recv()

    loop(nb, lambda e: rs_copy(e).start(), b)

    order = iota((256, 256), 1) == iota((256, 256), 0) % 128 * 2 + iota((256, 256), 0) // 128
    order = order.astype(jnp.float32).astype(jnp.bfloat16)

    def transform(g):
        halves = []
        for h in range(2):
            mixed = xv[pl.ds(h * 128, 128), g].reshape(256, length)
            halves.append(
                jnp.dot(order, mixed, preferred_element_type=jnp.float32).astype(jnp.bfloat16)
            )
        for v in range(2):
            m = g * 2 + v
            rows = jnp.concatenate([half[v * 128:(v + 1) * 128] for half in halves], axis=0)
            spectrum = lax.dot_general(ftv[...], rows, NT, preferred_element_type=jnp.float32)
            w[m] = spectrum
            energy = jnp.sum(spectrum * spectrum, axis=0, keepdims=True) * (1.0 / length)
            scale[m] = lax.rsqrt(energy + 1e-06) * valid[g, pl.ds(v, 1), :].astype(jnp.float32)

    def transforms(low, high):
        def step(g, _):
            transform(g)
            return 0

        lax.fori_loop(low, high, step, 0)

    pltpu.make_async_copy(ft_hbm, ftv, ft_sem).wait()
    transforms(0, 2)

    rsb[b] = slab[part, core]
    loop(nb, rs_arrived, b)
    shape = (m_count * 2 * NP, nb * 32)
    row, lane = iota(shape, 0), iota(shape, 1)
    wanted = jnp.zeros(shape, jnp.int32)
    for panel in range(NP):
        wanted = jnp.where(row // 2 % NP == panel, owner[panel], wanted)
    choice = (
        (lane // 32 == wanted) & (lane // 16 % 2 == row % 2) & (lane % 16 == row // (2 * NP))
    )
    picked = jnp.dot(
        choice.astype(jnp.float32).astype(jnp.bfloat16), rsb[...].reshape(nb * 32, lanes),
        preferred_element_type=jnp.float32,
    )
    xs[part, core] = picked.astype(jnp.bfloat16)

    def ag_copy(r):
        return remote(xs.at[part, core], xs.at[part, core], ag_send.at[r],
                      ag_recv.at[part, core], (2 * r + core, t))

    def fw_copy(r):
        return remote(xs.at[r, core], xs.at[r, core], fw_send.at[r], ag_recv.at[r, core], sibling)

    def arrived(r, h):
        remote(xs.at[r, h], xs.at[r, h], fw_send.at[r], ag_recv.at[r, h], sibling).wait_recv()

    loop(nr, lambda r: ag_copy(r).start(), part)
    fw_copy(part).start()
    transforms(2, segments - 1)

    def forward(r):
        arrived(r, core)
        fw_copy(r).start()

    loop(nr, forward, part)
    transforms(segments - 1, segments)
    loop(nr, lambda r: arrived(r, 1 - core))

    half_rows = []
    for h in range(2):
        half_rows.append(jnp.concatenate([xs[r, h] for r in range(nr)], axis=1))
        half_rows.append(jnp.zeros((128 - m_count * 2 * NP, length), jnp.bfloat16))
    source_rows = jnp.concatenate(half_rows, axis=0)
    spectrum = lax.dot_general(ftv[...], source_rows, NT, preferred_element_type=jnp.float32)
    energy = jnp.sum(spectrum * spectrum, axis=0, keepdims=True) * (1.0 / length)
    s[...] = spectrum * lax.rsqrt(energy + 1e-06)


    def correlate_group(k0):
        row, lane = iota((128, 256), 0), iota((128, 256), 1)
        channel = lane // 2 % NP * PP + lane // 128 * 2 + lane % 2
        copies = (row // GB == channel).astype(jnp.float32).astype(jnp.bfloat16)
        segment = row // GB == lane // (2 * NP) % 16
        diagonal = row % GB == lane % GB
        stacked = []
        for base in (0, bins):
            tile = s[pl.ds(pl.multiple_of(base + k0, GB), GB), :]
            stacked.append(jnp.where(segment, jnp.concatenate([tile] * 16, axis=0), 0.0))
        stacked = jnp.concatenate(stacked, axis=0).astype(jnp.bfloat16)
        real = lax.dot_general(copies, stacked, NT, preferred_element_type=jnp.float32)
        real = jnp.where(diagonal, real, 0.0)
        imag = jnp.concatenate([-real[:, 128:], real[:, :128]], axis=1)
        left_side = jnp.concatenate([real, imag], axis=0).astype(jnp.bfloat16)
        rows = []
        for base in (0, bins):
            for m in range(m_count):
                tile = w[m, pl.ds(pl.multiple_of(base + k0, GB), GB), :]
                rows.append(tile * scale[m])
            rows.append(jnp.zeros((128 - m_count * GB, channels), jnp.float32))
        right_side = jnp.concatenate(rows, axis=0).astype(jnp.bfloat16)
        return jnp.dot(left_side, right_side, preferred_element_type=jnp.float32)

    def correlate_chunk(c):
        for g in range(GP):
            k0 = c * KB + g * PAIR
            first = correlate_group(k0).reshape(2, J, GB, channels)
            second = correlate_group(k0 + GB).reshape(2, J, GB, channels)
            both = jnp.concatenate([first, second], axis=2).astype(jnp.bfloat16)
            both = both.reshape(2, ny, 2, 2, PAIR, channels)
            for o in range(2):
                p[c, :, :, :, pl.ds((g * 2 + o) * PAIR, PAIR), :] = both[o]

    def z1(n):
        return remote(p.at[n, :, 1 - z], rz1.at[n], z1_send.at[n], z1_recv.at[n], across)

    def ring(parts, n, fl, fr, rl, rr, send, fl_recv, fr_recv, rl_recv, rr_recv):
        def copy(i):
            src, dst, recv, device = (
                lambda: (parts(yo, 0), fl.at[n], fl_recv.at[n], right),
                lambda: (parts(yo, 1), fr.at[n], fr_recv.at[n], left),
                lambda: (parts(yr, 1), rl.at[n, 1], rl_recv.at[n, 1], right),
                lambda: (parts(yl, 0), rr.at[n, 0], rr_recv.at[n, 0], left),
                lambda: (fl.at[n], rl.at[n, 0], rl_recv.at[n, 0], right),
                lambda: (fr.at[n], rr.at[n, 1], rr_recv.at[n, 1], left),
            )[i]()
            return remote(src, dst, send.at[n, i], recv, device)

        return copy

    def add(a, c):
        return (a.astype(jnp.float32) + c.astype(jnp.float32)).astype(jnp.bfloat16)

    def z_ring(n):
        return ring(lambda o, h: rz1.at[n, o, h], n, zfl, zfr, zrl, zrr,
                    zy_send, zfl_recv, zfr_recv, zrl_recv, zrr_recv)

    def y_ring(n):
        return ring(lambda o, h: p.at[NZ + n, o, h], n, yfl, yfr, yrl, yrr,
                    yy_send, yfl_recv, yfr_recv, yrl_recv, yrr_recv)

    def z2(n):
        return remote(zs.at[n], rz2.at[n], z2_send.at[n], z2_recv.at[n], across)

    def slot(n, _):
        @pl.when(n < NZ)
        def _():
            correlate_chunk(n)
            z1(n).start()

        @pl.when(n < NY)
        def _():
            correlate_chunk(NZ + n)
            for i in range(4):
                y_ring(n)(i).start()

        @pl.when((n >= 1) & (n < NY + 1))
        def _():
            k = n - 1
            copies = y_ring(k)
            copies(0).wait_recv()
            yfl[k] = add(yfl[k], p[NZ + k, yr, 0])
            copies(4).start()
            copies(1).wait_recv()
            yfr[k] = add(yfr[k], p[NZ + k, yl, 1])
            copies(5).start()

        @pl.when((n >= 1) & (n < NZ + 1))
        def _():
            k = n - 1
            z1(k).wait_recv()
            rz1[k] = add(rz1[k], p[k, :, z])
            for i in range(4):
                z_ring(k)(i).start()

        @pl.when((n >= 2) & (n < NY + 2))
        def _():
            k = n - 2
            copies = y_ring(k)
            for i in (2, 3, 4, 5):
                copies(i).wait_recv()
            total = (p[NZ + k, y].astype(jnp.float32) + yrl[k].astype(jnp.float32)
                     + yrr[k].astype(jnp.float32))
            zs[k] = jnp.where(z == 0, total[1], total[0]).astype(jnp.bfloat16)
            keep[k] = jnp.where(z == 0, total[0], total[1])
            z2(k).start()

        @pl.when((n >= 2) & (n < NZ + 2))
        def _():
            k = n - 2
            copies = z_ring(k)
            copies(0).wait_recv()
            zfl[k] = add(zfl[k], rz1[k, yr, 0])
            copies(4).start()
            copies(1).wait_recv()
            zfr[k] = add(zfr[k], rz1[k, yl, 1])
            copies(5).start()

        @pl.when((n >= 3) & (n < NZ + 3))
        def _():
            k = n - 3
            copies = z_ring(k)
            for i in (2, 3, 4, 5):
                copies(i).wait_recv()
            c_out[:, k] = (rz1[k, y].astype(jnp.float32) + zrl[k].astype(jnp.float32)
                           + zrr[k].astype(jnp.float32)).astype(jnp.bfloat16)

        @pl.when(n >= 3)
        def _():
            k = n - 3
            z2(k).wait_recv()
            c_out[:, NZ + k] = (keep[k] + rz2[k].astype(jnp.float32)).astype(jnp.bfloat16)

        return 0

    lax.fori_loop(0, NY + 3, slot, 0)

    loop(nb, lambda e: rs_copy(e).wait_send(), b)
    loop(nr, lambda r: ag_copy(r).wait_send(), part)
    loop(nr, lambda r: fw_copy(r).wait_send())

    def drain_z(n):
        z1(n).wait_send()
        for i in range(6):
            z_ring(n)(i).wait_send()

    def drain_y(n):
        z2(n).wait_send()
        for i in range(6):
            y_ring(n)(i).wait_send()

    loop(NZ, drain_z)
    loop(NY, drain_y)


def on_device(traces, valid, panel_owner, panel_start):
    channels, windows_here, segments, length = traces.shape
    m_count = windows_here * segments
    nb = lax.axis_size("block")
    nt = lax.axis_size("tm")
    nr = nb // 2
    ny = nt // 2
    lanes = length // nr
    forward = jnp.asarray(forward_t(length))
    inverse = jnp.asarray(
        inverse_rows(length, 1.0 / math.sqrt(length // 2 * m_count * nt))
    )
    bf16, f32 = jnp.bfloat16, jnp.float32
    dma = pltpu.SemaphoreType.DMA
    vmem = pl.BlockSpec(memory_space=pltpu.VMEM)
    hbm = pl.BlockSpec(memory_space=pl.ANY)
    smem = pl.BlockSpec(memory_space=pltpu.SMEM)
    chunks = NZ + NY
    unit = (RJ, channels)
    cross = pl.pallas_call(
        functools.partial(kernel, (nb, nt, segments, length)),
        out_shape=jax.ShapeDtypeStruct((2, chunks) + unit, bf16),
        in_specs=[hbm, hbm, vmem, smem, smem],
        out_specs=vmem,
        scratch_shapes=[
            pltpu.VMEM((channels, segments, windows_here, length), bf16),
            pltpu.VMEM((length, length), bf16),
            pltpu.VMEM((m_count, length, channels), f32),
            pltpu.VMEM((m_count, 1, channels), f32),
            pltpu.VMEM((chunks, ny, 2, 2) + unit, bf16),
            pltpu.VMEM((length, 256), f32),
            pltpu.VMEM((nr, 2, 32, lanes), bf16),
            pltpu.VMEM((nr, 2, m_count * 2 * NP, lanes), bf16),
            pltpu.VMEM((nb, 32, lanes), bf16),
            pltpu.VMEM((NY, 2) + unit, f32),
            pltpu.VMEM((NZ, ny, 2) + unit, bf16),
            pltpu.VMEM((NZ,) + unit, bf16),
            pltpu.VMEM((NZ,) + unit, bf16),
            pltpu.VMEM((NZ, 2) + unit, bf16),
            pltpu.VMEM((NZ, 2) + unit, bf16),
            pltpu.VMEM((NY, 2) + unit, bf16),
            pltpu.VMEM((NY, 2) + unit, bf16),
            pltpu.VMEM((NY, 2, 2) + unit, bf16),
            pltpu.VMEM((NY, 2, 2) + unit, bf16),
            pltpu.VMEM((NY, 2) + unit, bf16),
            pltpu.VMEM((NY, 2) + unit, bf16),
            dma((segments,)), dma, dma((nb,)), dma((nb,)), dma((nr,)), dma((nr,)), dma((nr, 2)),
            dma((NZ,)), dma((NZ,)),
            dma((NZ, 6)), dma((NZ,)), dma((NZ,)), dma((NZ, 2)), dma((NZ, 2)),
            dma((NY, 6)), dma((NY,)), dma((NY,)), dma((NY, 2)), dma((NY, 2)),
            dma((NY,)), dma((NY,)),
        ],
        compiler_params=pltpu.CompilerParams(
            collective_id=0, has_side_effects=True, vmem_limit_bytes=56 * 2**20
        ),
        name="cross",
    )(traces.transpose(0, 2, 1, 3), forward, valid.transpose(2, 1, 0), panel_owner, panel_start)
    cross = cross.reshape(2, length, channels)
    return lax.dot_general(
        cross, inverse, (((1,), (0,)), ((), ())), preferred_element_type=f32
    )


def solution(mesh):
    in_specs = (P("block", "tm", None, None), P("block", "tm", None), P(), P())
    out_specs = P("tm", "block", None)
    return jax.shard_map(
        on_device, mesh=mesh, in_specs=in_specs, out_specs=out_specs, check_vma=False
    )
```

```python
import functools
import math

import jax
import jax.numpy as jnp
import ml_dtypes
import numpy as np
from jax import lax
from jax.experimental import pallas as pl
from jax.experimental.pallas import tpu as pltpu
from jax.sharding import PartitionSpec as P

MESH = pl.DeviceIdType.MESH
PP = 4
NP = 4
J = PP * NP
GB = 8
PAIR = 2 * GB
KB = PAIR
RJ = 2 * PAIR
NY = 8
NW = 12
PB = 2 * KB
PIECES = NW * KB // PB
CAP = 1536
LAG = (2, 4, 6)
NT = (((1,), (1,)), ((), ()))


def forward_t(length):
    k = np.arange(length // 2)
    n = np.arange(length)
    a = (k[:, None] * n[None, :] % length) * (2.0 * math.pi / length)
    return np.concatenate([np.cos(a), -np.sin(a)], axis=0).astype(np.float32).astype(ml_dtypes.bfloat16)


def inverse_rows(length, factor):
    bins = length // 2
    k = np.arange(bins)
    t = np.arange(length)
    a = (k[:, None] * t[None, :] % length) * (2.0 * math.pi / length)
    w = np.where(k == 0, 1.0, 2.0)[:, None] * factor
    full = np.stack([w * np.cos(a), -w * np.sin(a)])
    full = full.reshape(2, bins // PAIR, PAIR, length).transpose(1, 0, 2, 3)
    return full.reshape(length, length).astype(np.float32).astype(ml_dtypes.bfloat16)


def kernel(dims, x_hbm, ft_hbm, valid, owner, first, c_out, xv, ftv, w, scale, p, s, slab, xs,
           rsb, valid2, pos, choose, choose2, pick, packed, packed2, w2, sb, sb2,
           keep, yfl, yfr, yrl, yrr, zs, rz2,
           x_sem, ft_sem, rs_send, rs_recv, ag_send, fw_send, ag_recv,
           v_send, v_recv, pk_send, pk_recv, sb_send, sb_recv,
           yy_send, yfl_recv, yfr_recv, yrl_recv, yrr_recv, z2_send, z2_recv):
    nb, nt, segments, length = dims
    m_count = 2 * segments
    bins = length // 2
    channels = c_out.shape[-1]
    ny = nt // 2
    nr = nb // 2
    lanes = length // nr
    b = lax.axis_index("block")
    t = lax.axis_index("tm")
    part = b // 2
    core = b % 2
    y = t // 2
    z = t % 2
    right = (b, (y + 1) % ny * 2 + z)
    left = (b, (y + ny - 1) % ny * 2 + z)
    across = (b, y * 2 + 1 - z)
    sibling = (part * 2 + 1 - core, t)
    yr = (y + 1) % ny
    yl = (y + ny - 1) % ny
    yo = (y + 2) % ny

    def remote(src, dst, send, recv, device):
        return pltpu.make_async_remote_copy(
            src_ref=src, dst_ref=dst, send_sem=send, recv_sem=recv,
            device_id=device, device_id_type=MESH,
        )

    def iota(shape, axis):
        return lax.broadcasted_iota(jnp.int32, shape, axis)

    def loop(count, body, skip=None):
        def step(i, _):
            if skip is None:
                body(i)
            else:
                pl.when(i != skip)(lambda: body(i))
            return 0

        lax.fori_loop(0, count, step, 0)

    def load(g):
        return pltpu.make_async_copy(x_hbm.at[:, g], xv.at[:, g], x_sem.at[g])

    loop(segments, lambda g: load(g).start())
    pltpu.make_async_copy(ft_hbm, ftv, ft_sem).start()

    barrier = pltpu.get_barrier_semaphore()

    def greet(device):
        pl.semaphore_signal(barrier, inc=1, device_id=device, device_id_type=MESH)

    loop(nb, lambda e: greet((e, t)), b)
    for device in (right, left, across):
        greet(device)

    loop(segments, lambda g: load(g).wait())
    start = 0
    for panel in range(NP):
        start = start + jnp.where(owner[panel] == b, first[panel], 0)
    valid_rows = valid[...].reshape(m_count, channels).astype(jnp.float32)
    for q in range(PP):
        good = jnp.sum(
            jnp.where(iota((m_count, channels), 1) == start + q, valid_rows, 0.0),
            axis=1, keepdims=True,
        )
        rows = xv[start + q].reshape(m_count, length).astype(jnp.float32) * good
        rows = jnp.concatenate([rows, jnp.zeros((16 - m_count, length), jnp.float32)], axis=0)
        rows = rows.astype(jnp.bfloat16)
        for r in range(nr):
            slab[r, q // 2, pl.ds(q % 2 * 16, 16), :] = rows[:, r * lanes:(r + 1) * lanes]
    pl.semaphore_wait(barrier, nb - 1 + 3)

    def rs_copy(e):
        return remote(slab.at[e // 2, e % 2], rsb.at[b], rs_send.at[e], rs_recv.at[b], (e, t))

    def rs_arrived(e):
        remote(slab.at[part, core], rsb.at[e], rs_send.at[e], rs_recv.at[e], (e, t)).wait_recv()

    loop(nb, lambda e: rs_copy(e).start(), b)
    v_copy = remote(valid, valid2, v_send, v_recv, across)
    v_copy.start()

    order = iota((256, 256), 1) == iota((256, 256), 0) % 128 * 2 + iota((256, 256), 0) // 128
    order = order.astype(jnp.float32).astype(jnp.bfloat16)

    def transform(g):
        halves = []
        for h in range(2):
            mixed = xv[pl.ds(h * 128, 128), g].reshape(256, length)
            halves.append(
                jnp.dot(order, mixed, preferred_element_type=jnp.float32).astype(jnp.bfloat16)
            )
        for v in range(2):
            m = g * 2 + v
            rows = jnp.concatenate([half[v * 128:(v + 1) * 128] for half in halves], axis=0)
            spectrum = lax.dot_general(ftv[...], rows, NT, preferred_element_type=jnp.float32)
            w[m] = spectrum
            energy = jnp.sum(spectrum * spectrum, axis=0, keepdims=True) * (1.0 / length)
            scale[m] = lax.rsqrt(energy + 1e-06) * valid[g, pl.ds(v, 1), :].astype(jnp.float32)

    def transforms(low, high):
        def step(g, _):
            transform(g)
            return 0

        lax.fori_loop(low, high, step, 0)

    pltpu.make_async_copy(ft_hbm, ftv, ft_sem).wait()
    transforms(0, 4)

    rsb[b] = slab[part, core]
    loop(nb, rs_arrived, b)
    shape = (m_count * 2 * NP, nb * 32)
    row, lane = iota(shape, 0), iota(shape, 1)
    wanted = jnp.zeros(shape, jnp.int32)
    for panel in range(NP):
        wanted = jnp.where(row // 2 % NP == panel, owner[panel], wanted)
    choice = (
        (lane // 32 == wanted) & (lane // 16 % 2 == row % 2) & (lane % 16 == row // (2 * NP))
    )
    picked = jnp.dot(
        choice.astype(jnp.float32).astype(jnp.bfloat16), rsb[...].reshape(nb * 32, lanes),
        preferred_element_type=jnp.float32,
    )
    xs[part, core] = picked.astype(jnp.bfloat16)

    def ag_copy(r):
        return remote(xs.at[part, core], xs.at[part, core], ag_send.at[r],
                      ag_recv.at[part, core], (2 * r + core, t))

    def fw_copy(r):
        return remote(xs.at[r, core], xs.at[r, core], fw_send.at[r], ag_recv.at[r, core], sibling)

    def arrived(r, h):
        remote(xs.at[r, h], xs.at[r, h], fw_send.at[r], ag_recv.at[r, h], sibling).wait_recv()

    loop(nr, lambda r: ag_copy(r).start(), part)
    fw_copy(part).start()
    transforms(4, segments)

    def forward(r):
        arrived(r, core)
        fw_copy(r).start()

    loop(nr, forward, part)

    places = CAP // 256

    def build(valid_ref, choose_ref):
        good = valid_ref[...].reshape(m_count, channels).astype(jnp.float32)
        good = jnp.concatenate([good, jnp.zeros((16 - m_count, channels), jnp.float32)], axis=0)
        narrow = good.astype(jnp.bfloat16)
        before = (iota((channels, channels), 0) < iota((channels, channels), 1))
        before = before.astype(jnp.float32).astype(jnp.bfloat16)
        rank = jnp.dot(narrow, before, preferred_element_type=jnp.float32)
        above = (iota((16, 16), 1) < iota((16, 16), 0)).astype(jnp.float32).astype(jnp.bfloat16)
        rank = rank + jnp.sum(
            jnp.dot(above, narrow, preferred_element_type=jnp.float32), axis=1, keepdims=True
        )
        rank = jnp.where(good > 0.0, rank, -1.0)
        for m in range(m_count):
            pos[m] = rank[m:m + 1]

        def body(m):
            number = iota((256, channels), 0).astype(jnp.float32)
            for c in range(places):
                hit = jnp.where(number + 256.0 * c == pos[m], 1.0, 0.0).astype(jnp.bfloat16)
                choose_ref[c, :, pl.ds(pl.multiple_of(m * channels, channels), channels)] = hit

        loop(m_count, body)

    def w_bin(half, i):
        return NY * KB + half * (NW * KB) + i * PB

    def pack(i):
        for m in range(m_count):
            rows = []
            for piece in range(2):
                for base in (0, bins):
                    k0 = pl.multiple_of(base + w_bin(1 - z, i + piece), PB)
                    rows.append(w[m, pl.ds(k0, PB), :] * scale[m])
            pick[:, m * channels:(m + 1) * channels] = (
                jnp.concatenate(rows, axis=0).astype(jnp.bfloat16)
            )

        def body(c):
            part_c = lax.dot_general(pick[...], choose[c], NT, preferred_element_type=jnp.float32)
            part_c = part_c.astype(jnp.bfloat16).reshape(2, 2 * PB, 256)
            packed[pl.ds(i, 2), :, pl.ds(pl.multiple_of(c * 256, 256), 256)] = part_c

        loop(places, body)

    def pk_copy(i):
        return remote(packed.at[i], packed2.at[i], pk_send.at[i], pk_recv.at[i], across)

    def sb_copy(i):
        return remote(sb.at[i], sb2.at[i], sb_send.at[i], sb_recv.at[i], across)

    build(valid, choose)
    pack(0)
    pk_copy(0).start()
    pk_copy(1).start()
    loop(nr, lambda r: arrived(r, 1 - core))

    half_rows = []
    for h in range(2):
        half_rows.append(jnp.concatenate([xs[r, h] for r in range(nr)], axis=1))
        half_rows.append(jnp.zeros((128 - m_count * 2 * NP, length), jnp.bfloat16))
    source_rows = jnp.concatenate(half_rows, axis=0)
    spectrum = lax.dot_general(ftv[...], source_rows, NT, preferred_element_type=jnp.float32)
    energy = jnp.sum(spectrum * spectrum, axis=0, keepdims=True) * (1.0 / length)
    s[...] = spectrum * lax.rsqrt(energy + 1e-06)

    def narrow_sources(i):
        for o, base in enumerate((0, bins)):
            k0 = pl.multiple_of(base + w_bin(1 - z, i), PB)
            sb[i, o] = s[pl.ds(k0, PB), :].astype(jnp.bfloat16)

    loop(PIECES, narrow_sources)
    sb_copy(0).start()
    sb_copy(1).start()


    def source_matrix(real_tile, imag_tile):
        row, lane = iota((128, 256), 0), iota((128, 256), 1)
        channel = lane // 2 % NP * PP + lane // 128 * 2 + lane % 2
        copies = (row // GB == channel).astype(jnp.float32).astype(jnp.bfloat16)
        segment = row // GB == lane // (2 * NP) % 16
        diagonal = row % GB == lane % GB
        stacked = jnp.concatenate(
            [jnp.where(segment, jnp.concatenate([tile] * 16, axis=0), 0.0)
             for tile in (real_tile, imag_tile)], axis=0,
        ).astype(jnp.bfloat16)
        real = lax.dot_general(copies, stacked, NT, preferred_element_type=jnp.float32)
        real = jnp.where(diagonal, real, 0.0)
        imag = jnp.concatenate([-real[:, 128:], real[:, :128]], axis=1)
        return jnp.concatenate([real, imag], axis=0).astype(jnp.bfloat16)

    def channel_matrix(tile):
        rows = []
        for o in range(2):
            rows += [tile(o, m) for m in range(m_count)]
            rows.append(jnp.zeros((128 - m_count * GB, channels), jnp.float32))
        return jnp.concatenate(rows, axis=0).astype(jnp.bfloat16)

    def own_tile(k0):
        def tile(o, m):
            return w[m, pl.ds(pl.multiple_of(o * bins + k0, GB), GB), :] * scale[m]

        return tile

    def own_source(o, k0):
        return s[pl.ds(pl.multiple_of(o * bins + k0, GB), GB), :]

    def store_chunk(n, groups):
        groups = [g.reshape(2, J, GB, channels) for g in groups]
        both = jnp.concatenate(groups, axis=2).astype(jnp.bfloat16)
        both = both.reshape(2, ny, 2, 2, PAIR, channels)
        for o in range(2):
            p[n, :, :, :, pl.ds(o * PAIR, PAIR), :] = both[o]

    def correlate_own(n):
        groups = []
        for g in range(2):
            k0 = n * KB + g * GB
            groups.append(jnp.dot(
                source_matrix(own_source(0, k0), own_source(1, k0)),
                channel_matrix(own_tile(k0)), preferred_element_type=jnp.float32,
            ))
        store_chunk(n, groups)

    def correlate_both(k):
        i, half = k // 2, k % 2
        far = [sb2[i, o, pl.ds(pl.multiple_of(half * PAIR, PAIR), PAIR), :].astype(jnp.float32)
               for o in range(2)]
        groups = []
        for g in range(2):
            k0 = w_bin(z, 0) + k * KB + g * GB
            near = source_matrix(own_source(0, k0), own_source(1, k0))
            other = source_matrix(*[f[g * GB:(g + 1) * GB] for f in far])

            def far_tile(o, m):
                row = (i % 2 * 2 + o) * PB + half * PAIR + g * GB
                return w2[m, pl.ds(pl.multiple_of(row, GB), GB), :]

            groups.append(jnp.dot(
                jnp.concatenate([near, other], axis=1),
                jnp.concatenate(
                    [channel_matrix(own_tile(k0)), channel_matrix(far_tile)], axis=0
                ),
                preferred_element_type=jnp.float32,
            ))
        store_chunk(NY + k, groups)

    def unpack(i):
        for piece in range(2):
            pk_copy(i + piece).wait_recv()
            sb_copy(i + piece).wait_recv()
        rows = packed2[pl.ds(i, 2)].reshape(4 * PB, CAP)

        def body(m):
            lanes_m = pl.ds(pl.multiple_of(m * channels, channels), channels)
            side = choose2[:, :, lanes_m].reshape(CAP, channels)
            w2[m] = jnp.dot(rows, side, preferred_element_type=jnp.float32)

        loop(m_count, body)

    def ring(n):
        def copy(i):
            src, dst, recv, device = (
                lambda: (p.at[n, yo, 0], yfl.at[n], yfl_recv.at[n], right),
                lambda: (p.at[n, yo, 1], yfr.at[n], yfr_recv.at[n], left),
                lambda: (p.at[n, yr, 1], yrl.at[n, 1], yrl_recv.at[n, 1], right),
                lambda: (p.at[n, yl, 0], yrr.at[n, 0], yrr_recv.at[n, 0], left),
                lambda: (yfl.at[n], yrl.at[n, 0], yrl_recv.at[n, 0], right),
                lambda: (yfr.at[n], yrr.at[n, 1], yrr_recv.at[n, 1], left),
            )[i]()
            return remote(src, dst, yy_send.at[n, i], recv, device)

        return copy

    def add(a, c):
        return (a.astype(jnp.float32) + c.astype(jnp.float32)).astype(jnp.bfloat16)

    def z2(n):
        return remote(zs.at[n], rz2.at[n], z2_send.at[n], z2_recv.at[n], across)

    def ring_pass(n):
        copies = ring(n)
        copies(0).wait_recv()
        yfl[n] = add(yfl[n], p[n, yr, 0])
        copies(4).start()
        copies(1).wait_recv()
        yfr[n] = add(yfr[n], p[n, yl, 1])
        copies(5).start()

    def ring_sum(n):
        copies = ring(n)
        for i in (2, 3, 4, 5):
            copies(i).wait_recv()
        total = (p[n, y].astype(jnp.float32) + yrl[n].astype(jnp.float32)
                 + yrr[n].astype(jnp.float32))
        zs[n] = jnp.where(z == 0, total[1], total[0]).astype(jnp.bfloat16)
        z2(n).start()
        mine = jnp.where(z == 0, total[0], total[1])

        @pl.when(n < NY)
        def _():
            keep[n] = mine

        @pl.when(n >= NY)
        def _():
            c_out[:, n + z * NW] = mine.astype(jnp.bfloat16)

    def ring_end(n):
        z2(n).wait_recv()

        @pl.when(n < NY)
        def _():
            c_out[:, n] = (keep[n] + rz2[n].astype(jnp.float32)).astype(jnp.bfloat16)

        @pl.when(n >= NY)
        def _():
            c_out[:, n + (1 - z) * NW] = rz2[n]

    def pack_rest(j):
        i = 2 * j + 2
        pack(i)
        for piece in range(2):
            pk_copy(i + piece).start()
            sb_copy(i + piece).start()

    chunks = NY + NW

    def slot(n, _):
        def at(lag, body):
            pl.when((n >= lag) & (n < chunks + lag))(lambda: body(n - lag))

        at(LAG[0], ring_pass)
        at(LAG[1], ring_sum)
        at(LAG[2], ring_end)

        @pl.when(n == 2)
        def _():
            loop(PIECES // 2 - 1, pack_rest)

        @pl.when(n == NY - 2)
        def _():
            v_copy.wait_recv()
            build(valid2, choose2)

        @pl.when(n < NY)
        def _():
            correlate_own(n)

        @pl.when((n >= NY) & (n < chunks) & ((n - NY) % 4 == 0))
        def _():
            unpack((n - NY) // 2)

        @pl.when((n >= NY) & (n < chunks))
        def _():
            correlate_both(n - NY)

        @pl.when(n < chunks)
        def _():
            for i in range(4):
                ring(n)(i).start()

        return 0

    lax.fori_loop(0, chunks + max(LAG), slot, 0)

    loop(nb, lambda e: rs_copy(e).wait_send(), b)
    loop(nr, lambda r: ag_copy(r).wait_send(), part)
    loop(nr, lambda r: fw_copy(r).wait_send())

    v_copy.wait_send()

    def drain_piece(i):
        pk_copy(i).wait_send()
        sb_copy(i).wait_send()

    loop(PIECES, drain_piece)

    def drain(n):
        z2(n).wait_send()
        for i in range(6):
            ring(n)(i).wait_send()

    loop(chunks, drain)


def on_device(traces, valid, panel_owner, panel_start):
    channels, windows_here, segments, length = traces.shape
    m_count = windows_here * segments
    nb = lax.axis_size("block")
    nt = lax.axis_size("tm")
    nr = nb // 2
    ny = nt // 2
    lanes = length // nr
    forward = jnp.asarray(forward_t(length))
    inverse = jnp.asarray(
        inverse_rows(length, 1.0 / math.sqrt(length // 2 * m_count * nt))
    )
    bf16, f32 = jnp.bfloat16, jnp.float32
    dma = pltpu.SemaphoreType.DMA
    vmem = pl.BlockSpec(memory_space=pltpu.VMEM)
    hbm = pl.BlockSpec(memory_space=pl.ANY)
    smem = pl.BlockSpec(memory_space=pltpu.SMEM)
    chunks = NY + 2 * NW
    work = NY + NW
    unit = (RJ, channels)
    cross = pl.pallas_call(
        functools.partial(kernel, (nb, nt, segments, length)),
        out_shape=jax.ShapeDtypeStruct((2, chunks) + unit, bf16),
        in_specs=[hbm, hbm, vmem, smem, smem],
        out_specs=vmem,
        scratch_shapes=[
            pltpu.VMEM((channels, segments, windows_here, length), bf16),
            pltpu.VMEM((length, length), bf16),
            pltpu.VMEM((m_count, length, channels), f32),
            pltpu.VMEM((m_count, 1, channels), f32),
            pltpu.VMEM((work, ny, 2, 2) + unit, bf16),
            pltpu.VMEM((length, 256), f32),
            pltpu.VMEM((nr, 2, 32, lanes), bf16),
            pltpu.VMEM((nr, 2, m_count * 2 * NP, lanes), bf16),
            pltpu.VMEM((nb, 32, lanes), bf16),
            pltpu.VMEM((segments, windows_here, channels), jnp.int32),
            pltpu.VMEM((m_count, 1, channels), f32),
            pltpu.VMEM((CAP // 256, 256, m_count * channels), bf16),
            pltpu.VMEM((CAP // 256, 256, m_count * channels), bf16),
            pltpu.VMEM((4 * PB, m_count * channels), bf16),
            pltpu.VMEM((PIECES, 2 * PB, CAP), bf16),
            pltpu.VMEM((PIECES, 2 * PB, CAP), bf16),
            pltpu.VMEM((m_count, 4 * PB, channels), f32),
            pltpu.VMEM((PIECES, 2, PB, 256), bf16),
            pltpu.VMEM((PIECES, 2, PB, 256), bf16),
            pltpu.VMEM((NY, 2) + unit, f32),
            pltpu.VMEM((work, 2) + unit, bf16),
            pltpu.VMEM((work, 2) + unit, bf16),
            pltpu.VMEM((work, 2, 2) + unit, bf16),
            pltpu.VMEM((work, 2, 2) + unit, bf16),
            pltpu.VMEM((work, 2) + unit, bf16),
            pltpu.VMEM((work, 2) + unit, bf16),
            dma((segments,)), dma, dma((nb,)), dma((nb,)), dma((nr,)), dma((nr,)), dma((nr, 2)),
            dma, dma, dma((PIECES,)), dma((PIECES,)), dma((PIECES,)), dma((PIECES,)),
            dma((work, 6)), dma((work,)), dma((work,)), dma((work, 2)), dma((work, 2)),
            dma((work,)), dma((work,)),
        ],
        compiler_params=pltpu.CompilerParams(
            collective_id=0, has_side_effects=True, vmem_limit_bytes=60 * 2**20
        ),
        name="cross",
    )(traces.transpose(0, 2, 1, 3), forward, valid.transpose(2, 1, 0), panel_owner, panel_start)
    cross = cross.reshape(2, length, channels)
    return lax.dot_general(
        cross, inverse, (((1,), (0,)), ((), ())), preferred_element_type=f32
    )


def solution(mesh):
    in_specs = (P("block", "tm", None, None), P("block", "tm", None), P(), P())
    out_specs = P("tm", "block", None)
    return jax.shard_map(
        on_device, mesh=mesh, in_specs=in_specs, out_specs=out_specs, check_vma=False
    )
```

```python
import functools
import math

import jax
import jax.numpy as jnp
import ml_dtypes
import numpy as np
from jax import lax
from jax.experimental import pallas as pl
from jax.experimental.pallas import tpu as pltpu
from jax.sharding import PartitionSpec as P

MESH = pl.DeviceIdType.MESH
PP = 4
NP = 4
J = PP * NP
GB = 8
PAIR = 2 * GB
KB = PAIR
RJ = 2 * PAIR
NY = 4
NW = 14
PB = 2 * KB
PIECES = NW * KB // PB
CAP = 1536
LAG = (3, 6, 20)
NT = (((1,), (1,)), ((), ()))


def forward_t(length):
    k = np.arange(length // 2)
    n = np.arange(length)
    a = (k[:, None] * n[None, :] % length) * (2.0 * math.pi / length)
    return np.concatenate([np.cos(a), -np.sin(a)], axis=0).astype(np.float32).astype(ml_dtypes.bfloat16)


def inverse_rows(length, factor):
    bins = length // 2
    k = np.arange(bins)
    t = np.arange(length)
    a = (k[:, None] * t[None, :] % length) * (2.0 * math.pi / length)
    w = np.where(k == 0, 1.0, 2.0)[:, None] * factor
    full = np.stack([w * np.cos(a), -w * np.sin(a)])
    full = full.reshape(2, bins // PAIR, PAIR, length).transpose(1, 0, 2, 3)
    return full.reshape(length, length).astype(np.float32).astype(ml_dtypes.bfloat16)


def kernel(dims, x_hbm, ft_hbm, valid, owner, first, c_out, xv, ftv, w, scale, p, s, slab, xs,
           rsb, valid2, pos, choose, choose2, pick, packed, packed2, w2, sb, sb2,
           keep, yfl, yfr, yrl, yrr, zs, rz2,
           x_sem, ft_sem, rs_send, rs_recv, ag_send, fw_send, ag_recv,
           v_send, v_recv, pk_send, pk_recv, sb_send, sb_recv,
           yy_send, yfl_recv, yfr_recv, yrl_recv, yrr_recv, z2_send, z2_recv):
    nb, nt, segments, length = dims
    m_count = 2 * segments
    bins = length // 2
    channels = c_out.shape[-1]
    ny = nt // 2
    nr = nb // 2
    lanes = length // nr
    b = lax.axis_index("block")
    t = lax.axis_index("tm")
    part = b // 2
    core = b % 2
    y = t // 2
    z = t % 2
    right = (b, (y + 1) % ny * 2 + z)
    left = (b, (y + ny - 1) % ny * 2 + z)
    across = (b, y * 2 + 1 - z)
    sibling = (part * 2 + 1 - core, t)
    yr = (y + 1) % ny
    yl = (y + ny - 1) % ny
    yo = (y + 2) % ny

    def remote(src, dst, send, recv, device):
        return pltpu.make_async_remote_copy(
            src_ref=src, dst_ref=dst, send_sem=send, recv_sem=recv,
            device_id=device, device_id_type=MESH,
        )

    def iota(shape, axis):
        return lax.broadcasted_iota(jnp.int32, shape, axis)

    def loop(count, body, skip=None):
        def step(i, _):
            if skip is None:
                body(i)
            else:
                pl.when(i != skip)(lambda: body(i))
            return 0

        lax.fori_loop(0, count, step, 0)

    def load(g):
        return pltpu.make_async_copy(x_hbm.at[:, g], xv.at[:, g], x_sem.at[g])

    loop(segments, lambda g: load(g).start())
    pltpu.make_async_copy(ft_hbm, ftv, ft_sem).start()

    barrier = pltpu.get_barrier_semaphore()

    def greet(device):
        pl.semaphore_signal(barrier, inc=1, device_id=device, device_id_type=MESH)

    loop(nb, lambda e: greet((e, t)), b)
    for device in (right, left, across):
        greet(device)

    loop(segments, lambda g: load(g).wait())
    start = 0
    for panel in range(NP):
        start = start + jnp.where(owner[panel] == b, first[panel], 0)
    valid_rows = valid[...].reshape(m_count, channels).astype(jnp.float32)
    for q in range(PP):
        good = jnp.sum(
            jnp.where(iota((m_count, channels), 1) == start + q, valid_rows, 0.0),
            axis=1, keepdims=True,
        )
        rows = xv[start + q].reshape(m_count, length).astype(jnp.float32) * good
        rows = jnp.concatenate([rows, jnp.zeros((16 - m_count, length), jnp.float32)], axis=0)
        rows = rows.astype(jnp.bfloat16)
        for r in range(nr):
            slab[r, q // 2, pl.ds(q % 2 * 16, 16), :] = rows[:, r * lanes:(r + 1) * lanes]
    pl.semaphore_wait(barrier, nb - 1 + 3)

    def rs_copy(e):
        return remote(slab.at[e // 2, e % 2], rsb.at[b], rs_send.at[e], rs_recv.at[b], (e, t))

    def rs_arrived(e):
        remote(slab.at[part, core], rsb.at[e], rs_send.at[e], rs_recv.at[e], (e, t)).wait_recv()

    loop(nb, lambda e: rs_copy(e).start(), b)
    v_copy = remote(valid, valid2, v_send, v_recv, across)
    v_copy.start()

    order = iota((256, 256), 1) == iota((256, 256), 0) % 128 * 2 + iota((256, 256), 0) // 128
    order = order.astype(jnp.float32).astype(jnp.bfloat16)

    def transform(g):
        halves = []
        for h in range(2):
            mixed = xv[pl.ds(h * 128, 128), g].reshape(256, length)
            halves.append(
                jnp.dot(order, mixed, preferred_element_type=jnp.float32).astype(jnp.bfloat16)
            )
        for v in range(2):
            m = g * 2 + v
            rows = jnp.concatenate([half[v * 128:(v + 1) * 128] for half in halves], axis=0)
            spectrum = lax.dot_general(ftv[...], rows, NT, preferred_element_type=jnp.float32)
            w[m] = spectrum
            energy = jnp.sum(spectrum * spectrum, axis=0, keepdims=True) * (1.0 / length)
            scale[m] = lax.rsqrt(energy + 1e-06) * valid[g, pl.ds(v, 1), :].astype(jnp.float32)

    def transforms(low, high):
        def step(g, _):
            transform(g)
            return 0

        lax.fori_loop(low, high, step, 0)

    pltpu.make_async_copy(ft_hbm, ftv, ft_sem).wait()
    transforms(0, 4)

    rsb[b] = slab[part, core]
    loop(nb, rs_arrived, b)
    shape = (m_count * 2 * NP, nb * 32)
    row, lane = iota(shape, 0), iota(shape, 1)
    wanted = jnp.zeros(shape, jnp.int32)
    for panel in range(NP):
        wanted = jnp.where(row // 2 % NP == panel, owner[panel], wanted)
    choice = (
        (lane // 32 == wanted) & (lane // 16 % 2 == row % 2) & (lane % 16 == row // (2 * NP))
    )
    picked = jnp.dot(
        choice.astype(jnp.float32).astype(jnp.bfloat16), rsb[...].reshape(nb * 32, lanes),
        preferred_element_type=jnp.float32,
    )
    xs[part, core] = picked.astype(jnp.bfloat16)

    def ag_copy(r):
        return remote(xs.at[part, core], xs.at[part, core], ag_send.at[r],
                      ag_recv.at[part, core], (2 * r + core, t))

    def fw_copy(r):
        return remote(xs.at[r, core], xs.at[r, core], fw_send.at[r], ag_recv.at[r, core], sibling)

    def arrived(r, h):
        remote(xs.at[r, h], xs.at[r, h], fw_send.at[r], ag_recv.at[r, h], sibling).wait_recv()

    loop(nr, lambda r: ag_copy(r).start(), part)
    fw_copy(part).start()
    transforms(4, segments)

    def forward(r):
        arrived(r, core)
        fw_copy(r).start()

    loop(nr, forward, part)

    places = CAP // 256

    def build(valid_ref, choose_ref):
        good = valid_ref[...].reshape(m_count, channels).astype(jnp.float32)
        good = jnp.concatenate([good, jnp.zeros((16 - m_count, channels), jnp.float32)], axis=0)
        narrow = good.astype(jnp.bfloat16)
        before = (iota((channels, channels), 0) < iota((channels, channels), 1))
        before = before.astype(jnp.float32).astype(jnp.bfloat16)
        rank = jnp.dot(narrow, before, preferred_element_type=jnp.float32)
        above = (iota((16, 16), 1) < iota((16, 16), 0)).astype(jnp.float32).astype(jnp.bfloat16)
        rank = rank + jnp.sum(
            jnp.dot(above, narrow, preferred_element_type=jnp.float32), axis=1, keepdims=True
        )
        rank = jnp.where(good > 0.0, rank, -1.0)
        for m in range(m_count):
            pos[m] = rank[m:m + 1]

        def body(m):
            number = iota((256, channels), 0).astype(jnp.float32)
            for c in range(places):
                hit = jnp.where(number + 256.0 * c == pos[m], 1.0, 0.0).astype(jnp.bfloat16)
                choose_ref[c, :, pl.ds(pl.multiple_of(m * channels, channels), channels)] = hit

        loop(m_count, body)

    def w_bin(half, i):
        return NY * KB + half * (NW * KB) + i * PB

    def pack(i, count):
        for m in range(m_count):
            rows = []
            for piece in range(count):
                for base in (0, bins):
                    k0 = pl.multiple_of(base + w_bin(1 - z, i + piece), PB)
                    rows.append(w[m, pl.ds(k0, PB), :] * scale[m])
            pick[0:count * 2 * PB, m * channels:(m + 1) * channels] = (
                jnp.concatenate(rows, axis=0).astype(jnp.bfloat16)
            )

        def body(c):
            part_c = lax.dot_general(
                pick[0:count * 2 * PB, :], choose[c], NT, preferred_element_type=jnp.float32
            )
            part_c = part_c.astype(jnp.bfloat16).reshape(count, 2 * PB, 256)
            packed[i:i + count, :, pl.ds(pl.multiple_of(c * 256, 256), 256)] = part_c

        loop(places, body)

    def pk_copy(i):
        return remote(packed.at[i], packed2.at[i], pk_send.at[i], pk_recv.at[i], across)

    def sb_copy(i):
        return remote(sb.at[i], sb2.at[i], sb_send.at[i], sb_recv.at[i], across)

    build(valid, choose)
    pack(0, 2)
    pk_copy(0).start()
    pk_copy(1).start()
    loop(nr, lambda r: arrived(r, 1 - core))

    half_rows = []
    for h in range(2):
        half_rows.append(jnp.concatenate([xs[r, h] for r in range(nr)], axis=1))
        half_rows.append(jnp.zeros((128 - m_count * 2 * NP, length), jnp.bfloat16))
    source_rows = jnp.concatenate(half_rows, axis=0)
    spectrum = lax.dot_general(ftv[...], source_rows, NT, preferred_element_type=jnp.float32)
    energy = jnp.sum(spectrum * spectrum, axis=0, keepdims=True) * (1.0 / length)
    s[...] = spectrum * lax.rsqrt(energy + 1e-06)

    def narrow_sources(i):
        for o, base in enumerate((0, bins)):
            k0 = pl.multiple_of(base + w_bin(1 - z, i), PB)
            sb[i, o] = s[pl.ds(k0, PB), :].astype(jnp.bfloat16)

    loop(PIECES, narrow_sources)
    sb_copy(0).start()
    sb_copy(1).start()


    def source_matrix(real_tile, imag_tile):
        row, lane = iota((128, 256), 0), iota((128, 256), 1)
        channel = lane // 2 % NP * PP + lane // 128 * 2 + lane % 2
        copies = (row // GB == channel).astype(jnp.float32).astype(jnp.bfloat16)
        segment = row // GB == lane // (2 * NP) % 16
        diagonal = row % GB == lane % GB
        stacked = jnp.concatenate(
            [jnp.where(segment, jnp.concatenate([tile] * 16, axis=0), 0.0)
             for tile in (real_tile, imag_tile)], axis=0,
        ).astype(jnp.bfloat16)
        real = lax.dot_general(copies, stacked, NT, preferred_element_type=jnp.float32)
        real = jnp.where(diagonal, real, 0.0)
        imag = jnp.concatenate([-real[:, 128:], real[:, :128]], axis=1)
        return jnp.concatenate([real, imag], axis=0).astype(jnp.bfloat16)

    def channel_matrix(tile):
        rows = []
        for o in range(2):
            rows += [tile(o, m) for m in range(m_count)]
            rows.append(jnp.zeros((128 - m_count * GB, channels), jnp.float32))
        return jnp.concatenate(rows, axis=0).astype(jnp.bfloat16)

    def own_tile(k0):
        def tile(o, m):
            return w[m, pl.ds(pl.multiple_of(o * bins + k0, GB), GB), :] * scale[m]

        return tile

    def own_source(o, k0):
        return s[pl.ds(pl.multiple_of(o * bins + k0, GB), GB), :]

    def store_chunk(n, groups):
        groups = [g.reshape(2, J, GB, channels) for g in groups]
        both = jnp.concatenate(groups, axis=2).astype(jnp.bfloat16)
        both = both.reshape(2, ny, 2, 2, PAIR, channels)
        for o in range(2):
            p[n, :, :, :, pl.ds(o * PAIR, PAIR), :] = both[o]

    def correlate_own(n):
        groups = []
        for g in range(2):
            k0 = n * KB + g * GB
            groups.append(jnp.dot(
                source_matrix(own_source(0, k0), own_source(1, k0)),
                channel_matrix(own_tile(k0)), preferred_element_type=jnp.float32,
            ))
        store_chunk(n, groups)

    def correlate_both(k):
        i, half = k // 2, k % 2
        far = [sb2[i, o, pl.ds(pl.multiple_of(half * PAIR, PAIR), PAIR), :].astype(jnp.float32)
               for o in range(2)]
        groups = []
        for g in range(2):
            k0 = w_bin(z, 0) + k * KB + g * GB
            near = source_matrix(own_source(0, k0), own_source(1, k0))
            other = source_matrix(*[f[g * GB:(g + 1) * GB] for f in far])

            def far_tile(o, m):
                row = ((i + 1) % 2 * 2 + o) * PB + half * PAIR + g * GB
                return w2[m, pl.ds(pl.multiple_of(row, GB), GB), :]

            groups.append(jnp.dot(
                jnp.concatenate([near, other], axis=1),
                jnp.concatenate(
                    [channel_matrix(own_tile(k0)), channel_matrix(far_tile)], axis=0
                ),
                preferred_element_type=jnp.float32,
            ))
        store_chunk(NY + k, groups)

    def unpack(i, count):
        for piece in range(count):
            pk_copy(i + piece).wait_recv()
            sb_copy(i + piece).wait_recv()
        rows = packed2[pl.ds(i, count)].reshape(count * 2 * PB, CAP)

        def body(m):
            lanes_m = pl.ds(pl.multiple_of(m * channels, channels), channels)
            side = choose2[:, :, lanes_m].reshape(CAP, channels)
            w2[m, (2 - count) * 2 * PB:4 * PB] = jnp.dot(
                rows, side, preferred_element_type=jnp.float32
            )

        loop(m_count, body)

    def ring(n):
        def copy(i):
            src, dst, recv, device = (
                lambda: (p.at[n, yo, 0], yfl.at[n], yfl_recv.at[n], right),
                lambda: (p.at[n, yo, 1], yfr.at[n], yfr_recv.at[n], left),
                lambda: (p.at[n, yr, 1], yrl.at[n, 1], yrl_recv.at[n, 1], right),
                lambda: (p.at[n, yl, 0], yrr.at[n, 0], yrr_recv.at[n, 0], left),
                lambda: (yfl.at[n], yrl.at[n, 0], yrl_recv.at[n, 0], right),
                lambda: (yfr.at[n], yrr.at[n, 1], yrr_recv.at[n, 1], left),
            )[i]()
            return remote(src, dst, yy_send.at[n, i], recv, device)

        return copy

    def add(a, c):
        return (a.astype(jnp.float32) + c.astype(jnp.float32)).astype(jnp.bfloat16)

    def z2(n):
        return remote(zs.at[n], rz2.at[n], z2_send.at[n], z2_recv.at[n], across)

    def ring_pass(n):
        copies = ring(n)
        copies(0).wait_recv()
        yfl[n] = add(yfl[n], p[n, yr, 0])
        copies(4).start()
        copies(1).wait_recv()
        yfr[n] = add(yfr[n], p[n, yl, 1])
        copies(5).start()

    def ring_sum(n):
        copies = ring(n)
        for i in (2, 3, 4, 5):
            copies(i).wait_recv()
        total = (p[n, y].astype(jnp.float32) + yrl[n].astype(jnp.float32)
                 + yrr[n].astype(jnp.float32))
        zs[n] = jnp.where(z == 0, total[1], total[0]).astype(jnp.bfloat16)
        z2(n).start()
        mine = jnp.where(z == 0, total[0], total[1])

        @pl.when(n < NY)
        def _():
            keep[n] = mine

        @pl.when(n >= NY)
        def _():
            c_out[:, n + z * NW] = mine.astype(jnp.bfloat16)

    def ring_end(n):
        z2(n).wait_recv()

        @pl.when(n < NY)
        def _():
            c_out[:, n] = (keep[n] + rz2[n].astype(jnp.float32)).astype(jnp.bfloat16)

        @pl.when(n >= NY)
        def _():
            c_out[:, n + (1 - z) * NW] = rz2[n]

    chunks = NY + NW

    def slot(n, _):
        def at(lag, body):
            pl.when((n >= lag) & (n < chunks + lag))(lambda: body(n - lag))

        @pl.when(n == NY - 1)
        def _():
            pack(2, PIECES - 2)
            for i in range(2, PIECES):
                pk_copy(i).start()
                sb_copy(i).start()

        at(LAG[0], ring_pass)
        at(LAG[1], ring_sum)
        at(LAG[2], ring_end)

        @pl.when(n == NY)
        def _():
            v_copy.wait_recv()
            build(valid2, choose2)

        @pl.when(n < NY)
        def _():
            correlate_own(n)

        @pl.when(n == NY)
        def _():
            unpack(0, 1)

        @pl.when((n > NY) & (n < chunks) & ((n - NY) % 4 == 2))
        def _():
            unpack((n - NY) // 2, 2)

        @pl.when((n >= NY) & (n < chunks))
        def _():
            correlate_both(n - NY)

        @pl.when(n < chunks)
        def _():
            for i in range(4):
                ring(n)(i).start()

        return 0

    lax.fori_loop(0, chunks + max(LAG), slot, 0)

    loop(nb, lambda e: rs_copy(e).wait_send(), b)
    loop(nr, lambda r: ag_copy(r).wait_send(), part)
    loop(nr, lambda r: fw_copy(r).wait_send())

    v_copy.wait_send()

    def drain_piece(i):
        pk_copy(i).wait_send()
        sb_copy(i).wait_send()

    loop(PIECES, drain_piece)

    def drain(n):
        z2(n).wait_send()
        for i in range(6):
            ring(n)(i).wait_send()

    loop(chunks, drain)


def on_device(traces, valid, panel_owner, panel_start):
    channels, windows_here, segments, length = traces.shape
    m_count = windows_here * segments
    nb = lax.axis_size("block")
    nt = lax.axis_size("tm")
    nr = nb // 2
    ny = nt // 2
    lanes = length // nr
    forward = jnp.asarray(forward_t(length))
    inverse = jnp.asarray(
        inverse_rows(length, 1.0 / math.sqrt(length // 2 * m_count * nt))
    )
    bf16, f32 = jnp.bfloat16, jnp.float32
    dma = pltpu.SemaphoreType.DMA
    vmem = pl.BlockSpec(memory_space=pltpu.VMEM)
    hbm = pl.BlockSpec(memory_space=pl.ANY)
    smem = pl.BlockSpec(memory_space=pltpu.SMEM)
    chunks = NY + 2 * NW
    work = NY + NW
    unit = (RJ, channels)
    cross = pl.pallas_call(
        functools.partial(kernel, (nb, nt, segments, length)),
        out_shape=jax.ShapeDtypeStruct((2, chunks) + unit, bf16),
        in_specs=[hbm, hbm, vmem, smem, smem],
        out_specs=vmem,
        scratch_shapes=[
            pltpu.VMEM((channels, segments, windows_here, length), bf16),
            pltpu.VMEM((length, length), bf16),
            pltpu.VMEM((m_count, length, channels), f32),
            pltpu.VMEM((m_count, 1, channels), f32),
            pltpu.VMEM((work, ny, 2, 2) + unit, bf16),
            pltpu.VMEM((length, 256), f32),
            pltpu.VMEM((nr, 2, 32, lanes), bf16),
            pltpu.VMEM((nr, 2, m_count * 2 * NP, lanes), bf16),
            pltpu.VMEM((nb, 32, lanes), bf16),
            pltpu.VMEM((segments, windows_here, channels), jnp.int32),
            pltpu.VMEM((m_count, 1, channels), f32),
            pltpu.VMEM((CAP // 256, 256, m_count * channels), bf16),
            pltpu.VMEM((CAP // 256, 256, m_count * channels), bf16),
            pltpu.VMEM(((PIECES - 2) * 2 * PB, m_count * channels), bf16),
            pltpu.VMEM((PIECES, 2 * PB, CAP), bf16),
            pltpu.VMEM((PIECES, 2 * PB, CAP), bf16),
            pltpu.VMEM((m_count, 4 * PB, channels), f32),
            pltpu.VMEM((PIECES, 2, PB, 256), bf16),
            pltpu.VMEM((PIECES, 2, PB, 256), bf16),
            pltpu.VMEM((NY, 2) + unit, f32),
            pltpu.VMEM((work, 2) + unit, bf16),
            pltpu.VMEM((work, 2) + unit, bf16),
            pltpu.VMEM((work, 2, 2) + unit, bf16),
            pltpu.VMEM((work, 2, 2) + unit, bf16),
            pltpu.VMEM((work, 2) + unit, bf16),
            pltpu.VMEM((work, 2) + unit, bf16),
            dma((segments,)), dma, dma((nb,)), dma((nb,)), dma((nr,)), dma((nr,)), dma((nr, 2)),
            dma, dma, dma((PIECES,)), dma((PIECES,)), dma((PIECES,)), dma((PIECES,)),
            dma((work, 6)), dma((work,)), dma((work,)), dma((work, 2)), dma((work, 2)),
            dma((work,)), dma((work,)),
        ],
        compiler_params=pltpu.CompilerParams(
            collective_id=0, has_side_effects=True, vmem_limit_bytes=60 * 2**20
        ),
        name="cross",
    )(traces.transpose(0, 2, 1, 3), forward, valid.transpose(2, 1, 0), panel_owner, panel_start)
    cross = cross.reshape(2, length, channels)
    return lax.dot_general(
        cross, inverse, (((1,), (0,)), ((), ())), preferred_element_type=f32
    )


def solution(mesh):
    in_specs = (P("block", "tm", None, None), P("block", "tm", None), P(), P())
    out_specs = P("tm", "block", None)
    return jax.shard_map(
        on_device, mesh=mesh, in_specs=in_specs, out_specs=out_specs, check_vma=False
    )
```

```python
import functools
import math

import jax
import jax.numpy as jnp
import ml_dtypes
import numpy as np
from jax import lax
from jax.experimental import pallas as pl
from jax.experimental.pallas import tpu as pltpu
from jax.sharding import PartitionSpec as P

MESH = pl.DeviceIdType.MESH
PP = 4
NP = 4
J = PP * NP
GB = 8
PAIR = 2 * GB
KB = PAIR
RJ = 2 * PAIR
NY = 8
NW = 12
PB = 2 * KB
PIECES = NW * KB // PB
CAP = 1536
LAG = (3, 6, 17)
NT = (((1,), (1,)), ((), ()))


def forward_t(length):
    k = np.arange(length // 2)
    n = np.arange(length)
    a = (k[:, None] * n[None, :] % length) * (2.0 * math.pi / length)
    return np.concatenate([np.cos(a), -np.sin(a)], axis=0).astype(np.float32).astype(ml_dtypes.bfloat16)


def inverse_rows(length, factor):
    bins = length // 2
    k = np.arange(bins)
    t = np.arange(length)
    a = (k[:, None] * t[None, :] % length) * (2.0 * math.pi / length)
    w = np.where(k == 0, 1.0, 2.0)[:, None] * factor
    full = np.stack([w * np.cos(a), -w * np.sin(a)])
    full = full.reshape(2, bins // PAIR, PAIR, length).transpose(1, 0, 2, 3)
    return full.reshape(length, length).astype(np.float32).astype(ml_dtypes.bfloat16)


def kernel(dims, x_hbm, ft_hbm, valid, owner, first, c_out, xv, ftv, w, scale, p, s, slab, xs,
           rsb, valid2, pos, choose, choose2, pick, packed, packed2, w2, sb, sb2,
           keep, yfl, yfr, yrl, yrr, zs, rz2,
           x_sem, ft_sem, rs_send, rs_recv, ag_send, fw_send, ag_recv,
           v_send, v_recv, pk_send, pk_recv, sb_send, sb_recv,
           yy_send, yfl_recv, yfr_recv, yrl_recv, yrr_recv, z2_send, z2_recv):
    nb, nt, segments, length = dims
    m_count = 2 * segments
    bins = length // 2
    channels = c_out.shape[-1]
    ny = nt // 2
    nr = nb // 2
    lanes = length // nr
    b = lax.axis_index("block")
    t = lax.axis_index("tm")
    part = b // 2
    core = b % 2
    y = t // 2
    z = t % 2
    right = (b, (y + 1) % ny * 2 + z)
    left = (b, (y + ny - 1) % ny * 2 + z)
    across = (b, y * 2 + 1 - z)
    sibling = (part * 2 + 1 - core, t)
    yr = (y + 1) % ny
    yl = (y + ny - 1) % ny
    yo = (y + 2) % ny

    def remote(src, dst, send, recv, device):
        return pltpu.make_async_remote_copy(
            src_ref=src, dst_ref=dst, send_sem=send, recv_sem=recv,
            device_id=device, device_id_type=MESH,
        )

    def iota(shape, axis):
        return lax.broadcasted_iota(jnp.int32, shape, axis)

    def loop(count, body, skip=None):
        def step(i, _):
            if skip is None:
                body(i)
            else:
                pl.when(i != skip)(lambda: body(i))
            return 0

        lax.fori_loop(0, count, step, 0)

    def load(g):
        return pltpu.make_async_copy(x_hbm.at[:, g], xv.at[:, g], x_sem.at[g])

    loop(segments, lambda g: load(g).start())
    pltpu.make_async_copy(ft_hbm, ftv, ft_sem).start()

    barrier = pltpu.get_barrier_semaphore()

    def greet(device):
        pl.semaphore_signal(barrier, inc=1, device_id=device, device_id_type=MESH)

    loop(nb, lambda e: greet((e, t)), b)
    for device in (right, left, across):
        greet(device)

    places = CAP // channels

    def lane_block(m):
        start = m * channels
        return pl.ds(start if isinstance(m, int) else pl.multiple_of(start, channels), channels)

    def by_segment(body):
        for m in range(places - 1):
            body(m, m + 1)

        def step(m, _):
            body(m, places)
            return 0

        lax.fori_loop(places - 1, m_count, step, 0)

    def build(valid_ref, choose_ref):
        good = valid_ref[...].reshape(m_count, channels).astype(jnp.float32)
        good = jnp.concatenate([good, jnp.zeros((16 - m_count, channels), jnp.float32)], axis=0)
        narrow = good.astype(jnp.bfloat16)
        before = (iota((channels, channels), 0) < iota((channels, channels), 1))
        before = before.astype(jnp.float32).astype(jnp.bfloat16)
        rank = jnp.dot(narrow, before, preferred_element_type=jnp.float32)
        above = (iota((16, 16), 1) < iota((16, 16), 0)).astype(jnp.float32).astype(jnp.bfloat16)
        rank = rank + jnp.sum(
            jnp.dot(above, narrow, preferred_element_type=jnp.float32), axis=1, keepdims=True
        )
        rank = jnp.where(good > 0.0, rank, -1.0)
        for m in range(m_count):
            pos[m] = rank[m:m + 1]

        number = iota((256, channels), 0).astype(jnp.float32)

        def fill(m, count):
            for c in range(count):
                hit = jnp.where(number + 256.0 * c == pos[m], 1.0, 0.0).astype(jnp.bfloat16)
                choose_ref[c, :, lane_block(m)] = hit

        by_segment(fill)

    build(valid, choose)

    loop(segments, lambda g: load(g).wait())
    start = 0
    for panel in range(NP):
        start = start + jnp.where(owner[panel] == b, first[panel], 0)
    valid_rows = valid[...].reshape(m_count, channels).astype(jnp.float32)
    for q in range(PP):
        good = jnp.sum(
            jnp.where(iota((m_count, channels), 1) == start + q, valid_rows, 0.0),
            axis=1, keepdims=True,
        )
        rows = xv[start + q].reshape(m_count, length).astype(jnp.float32) * good
        rows = jnp.concatenate([rows, jnp.zeros((16 - m_count, length), jnp.float32)], axis=0)
        rows = rows.astype(jnp.bfloat16)
        for r in range(nr):
            slab[r, q // 2, pl.ds(q % 2 * 16, 16), :] = rows[:, r * lanes:(r + 1) * lanes]
    pl.semaphore_wait(barrier, nb - 1 + 3)

    def rs_copy(e):
        return remote(slab.at[e // 2, e % 2], rsb.at[b], rs_send.at[e], rs_recv.at[b], (e, t))

    def rs_arrived(e):
        remote(slab.at[part, core], rsb.at[e], rs_send.at[e], rs_recv.at[e], (e, t)).wait_recv()

    loop(nb, lambda e: rs_copy(e).start(), b)
    v_copy = remote(valid, valid2, v_send, v_recv, across)
    v_copy.start()

    order = iota((256, 256), 1) == iota((256, 256), 0) % 128 * 2 + iota((256, 256), 0) // 128
    order = order.astype(jnp.float32).astype(jnp.bfloat16)

    def transform(g):
        halves = []
        for h in range(2):
            mixed = xv[pl.ds(h * 128, 128), g].reshape(256, length)
            halves.append(
                jnp.dot(order, mixed, preferred_element_type=jnp.float32).astype(jnp.bfloat16)
            )
        for v in range(2):
            m = g * 2 + v
            rows = jnp.concatenate([half[v * 128:(v + 1) * 128] for half in halves], axis=0)
            spectrum = lax.dot_general(ftv[...], rows, NT, preferred_element_type=jnp.float32)
            w[m] = spectrum
            energy = jnp.sum(spectrum * spectrum, axis=0, keepdims=True) * (1.0 / length)
            scale[m] = lax.rsqrt(energy + 1e-06) * valid[g, pl.ds(v, 1), :].astype(jnp.float32)

    def transforms(low, high):
        def step(g, _):
            transform(g)
            return 0

        lax.fori_loop(low, high, step, 0)

    pltpu.make_async_copy(ft_hbm, ftv, ft_sem).wait()
    transforms(0, 4)

    rsb[b] = slab[part, core]
    loop(nb, rs_arrived, b)
    shape = (m_count * 2 * NP, nb * 32)
    row, lane = iota(shape, 0), iota(shape, 1)
    wanted = jnp.zeros(shape, jnp.int32)
    for panel in range(NP):
        wanted = jnp.where(row // 2 % NP == panel, owner[panel], wanted)
    choice = (
        (lane // 32 == wanted) & (lane // 16 % 2 == row % 2) & (lane % 16 == row // (2 * NP))
    )
    picked = jnp.dot(
        choice.astype(jnp.float32).astype(jnp.bfloat16), rsb[...].reshape(nb * 32, lanes),
        preferred_element_type=jnp.float32,
    )
    xs[part, core] = picked.astype(jnp.bfloat16)

    def ag_copy(r):
        return remote(xs.at[part, core], xs.at[part, core], ag_send.at[r],
                      ag_recv.at[part, core], (2 * r + core, t))

    def fw_copy(r):
        return remote(xs.at[r, core], xs.at[r, core], fw_send.at[r], ag_recv.at[r, core], sibling)

    def arrived(r, h):
        remote(xs.at[r, h], xs.at[r, h], fw_send.at[r], ag_recv.at[r, h], sibling).wait_recv()

    loop(nr, lambda r: ag_copy(r).start(), part)
    fw_copy(part).start()
    transforms(4, segments)

    def forward(r):
        arrived(r, core)
        fw_copy(r).start()

    loop(nr, forward, part)

    def w_bin(half, i):
        return NY * KB + half * (NW * KB) + i * PB

    def pack(i, count):
        for m in range(m_count):
            rows = []
            for piece in range(count):
                for base in (0, bins):
                    k0 = pl.multiple_of(base + w_bin(1 - z, i + piece), PB)
                    rows.append(w[m, pl.ds(k0, PB), :] * scale[m])
            pick[0:count * 2 * PB, m * channels:(m + 1) * channels] = (
                jnp.concatenate(rows, axis=0).astype(jnp.bfloat16)
            )

        for c in range(places):
            part_c = lax.dot_general(
                pick[0:count * 2 * PB, c * channels:], choose[c, :, c * channels:], NT,
                preferred_element_type=jnp.float32,
            )
            part_c = part_c.astype(jnp.bfloat16).reshape(count, 2 * PB, 256)
            packed[i:i + count, :, c * 256:(c + 1) * 256] = part_c

    def pk_copy(i):
        return remote(packed.at[i], packed2.at[i], pk_send.at[i], pk_recv.at[i], across)

    def sb_copy(i):
        return remote(sb.at[i], sb2.at[i], sb_send.at[i], sb_recv.at[i], across)

    pack(0, 2)
    pk_copy(0).start()
    pk_copy(1).start()
    loop(nr, lambda r: arrived(r, 1 - core))

    half_rows = []
    for h in range(2):
        half_rows.append(jnp.concatenate([xs[r, h] for r in range(nr)], axis=1))
        half_rows.append(jnp.zeros((128 - m_count * 2 * NP, length), jnp.bfloat16))
    source_rows = jnp.concatenate(half_rows, axis=0)
    spectrum = lax.dot_general(ftv[...], source_rows, NT, preferred_element_type=jnp.float32)
    energy = jnp.sum(spectrum * spectrum, axis=0, keepdims=True) * (1.0 / length)
    s[...] = spectrum * lax.rsqrt(energy + 1e-06)

    def narrow_sources(i):
        for o, base in enumerate((0, bins)):
            k0 = pl.multiple_of(base + w_bin(1 - z, i), PB)
            sb[i, o] = s[pl.ds(k0, PB), :].astype(jnp.bfloat16)

    loop(PIECES, narrow_sources)
    sb_copy(0).start()
    sb_copy(1).start()


    def source_matrix(real_tile, imag_tile):
        row, lane = iota((128, 256), 0), iota((128, 256), 1)
        channel = lane // 2 % NP * PP + lane // 128 * 2 + lane % 2
        copies = (row // GB == channel).astype(jnp.float32).astype(jnp.bfloat16)
        segment = row // GB == lane // (2 * NP) % 16
        diagonal = row % GB == lane % GB
        stacked = jnp.concatenate(
            [jnp.where(segment, jnp.concatenate([tile] * 16, axis=0), 0.0)
             for tile in (real_tile, imag_tile)], axis=0,
        ).astype(jnp.bfloat16)
        real = lax.dot_general(copies, stacked, NT, preferred_element_type=jnp.float32)
        real = jnp.where(diagonal, real, 0.0)
        imag = jnp.concatenate([-real[:, 128:], real[:, :128]], axis=1)
        return jnp.concatenate([real, imag], axis=0).astype(jnp.bfloat16)

    def channel_matrix(tile):
        rows = []
        for o in range(2):
            rows += [tile(o, m) for m in range(m_count)]
            rows.append(jnp.zeros((128 - m_count * GB, channels), jnp.float32))
        return jnp.concatenate(rows, axis=0).astype(jnp.bfloat16)

    def own_tile(k0):
        def tile(o, m):
            return w[m, pl.ds(pl.multiple_of(o * bins + k0, GB), GB), :] * scale[m]

        return tile

    def own_source(o, k0):
        return s[pl.ds(pl.multiple_of(o * bins + k0, GB), GB), :]

    def store_chunk(n, groups):
        groups = [g.reshape(2, J, GB, channels) for g in groups]
        both = jnp.concatenate(groups, axis=2).astype(jnp.bfloat16)
        both = both.reshape(2, ny, 2, 2, PAIR, channels)
        for o in range(2):
            p[n, :, :, :, pl.ds(o * PAIR, PAIR), :] = both[o]

    def correlate_own(n):
        groups = []
        for g in range(2):
            k0 = n * KB + g * GB
            groups.append(jnp.dot(
                source_matrix(own_source(0, k0), own_source(1, k0)),
                channel_matrix(own_tile(k0)), preferred_element_type=jnp.float32,
            ))
        store_chunk(n, groups)

    def correlate_both(k):
        i, half = k // 2, k % 2
        far = [sb2[i, o, pl.ds(pl.multiple_of(half * PAIR, PAIR), PAIR), :].astype(jnp.float32)
               for o in range(2)]
        groups = []
        for g in range(2):
            k0 = w_bin(z, 0) + k * KB + g * GB
            near = source_matrix(own_source(0, k0), own_source(1, k0))
            other = source_matrix(*[f[g * GB:(g + 1) * GB] for f in far])

            def far_tile(o, m):
                row = (i % 2 * 2 + o) * PB + half * PAIR + g * GB
                return w2[m, pl.ds(pl.multiple_of(row, GB), GB), :]

            groups.append(jnp.dot(
                jnp.concatenate([near, other], axis=1),
                jnp.concatenate(
                    [channel_matrix(own_tile(k0)), channel_matrix(far_tile)], axis=0
                ),
                preferred_element_type=jnp.float32,
            ))
        store_chunk(NY + k, groups)

    def unpack(i):
        for piece in range(2):
            pk_copy(i + piece).wait_recv()
            sb_copy(i + piece).wait_recv()
        rows = packed2[pl.ds(i, 2)].reshape(4 * PB, CAP)

        def body(m, count):
            lanes_m = lane_block(m)
            side = choose2[0:count, :, lanes_m].reshape(count * channels, channels)
            w2[m] = jnp.dot(
                rows[:, :count * channels], side, preferred_element_type=jnp.float32
            )

        by_segment(body)

    def ring(n):
        def copy(i):
            src, dst, recv, device = (
                lambda: (p.at[n, yo, 0], yfl.at[n], yfl_recv.at[n], right),
                lambda: (p.at[n, yo, 1], yfr.at[n], yfr_recv.at[n], left),
                lambda: (p.at[n, yr, 1], yrl.at[n, 1], yrl_recv.at[n, 1], right),
                lambda: (p.at[n, yl, 0], yrr.at[n, 0], yrr_recv.at[n, 0], left),
                lambda: (yfl.at[n], yrl.at[n, 0], yrl_recv.at[n, 0], right),
                lambda: (yfr.at[n], yrr.at[n, 1], yrr_recv.at[n, 1], left),
            )[i]()
            return remote(src, dst, yy_send.at[n, i], recv, device)

        return copy

    def add(a, c):
        return (a.astype(jnp.float32) + c.astype(jnp.float32)).astype(jnp.bfloat16)

    def z2(n):
        return remote(zs.at[n], rz2.at[n], z2_send.at[n], z2_recv.at[n], across)

    def ring_pass(n):
        copies = ring(n)
        copies(0).wait_recv()
        yfl[n] = add(yfl[n], p[n, yr, 0])
        copies(4).start()
        copies(1).wait_recv()
        yfr[n] = add(yfr[n], p[n, yl, 1])
        copies(5).start()

    def ring_sum(n):
        copies = ring(n)
        for i in (2, 3, 4, 5):
            copies(i).wait_recv()
        total = (p[n, y].astype(jnp.float32) + yrl[n].astype(jnp.float32)
                 + yrr[n].astype(jnp.float32))
        zs[n] = jnp.where(z == 0, total[1], total[0]).astype(jnp.bfloat16)
        z2(n).start()
        mine = jnp.where(z == 0, total[0], total[1])

        @pl.when(n < NY)
        def _():
            keep[n] = mine

        @pl.when(n >= NY)
        def _():
            c_out[:, n + z * NW] = mine.astype(jnp.bfloat16)

    def ring_end(n):
        z2(n).wait_recv()

        @pl.when(n < NY)
        def _():
            c_out[:, n] = (keep[n] + rz2[n].astype(jnp.float32)).astype(jnp.bfloat16)

        @pl.when(n >= NY)
        def _():
            c_out[:, n + (1 - z) * NW] = rz2[n]

    chunks = NY + NW

    def slot(n, _):
        def at(lag, body):
            pl.when((n >= lag) & (n < chunks + lag))(lambda: body(n - lag))

        @pl.when(n == NY // 2)
        def _():
            pack(2, PIECES - 2)
            for i in range(2, PIECES):
                pk_copy(i).start()
                sb_copy(i).start()

        at(LAG[0], ring_pass)
        at(LAG[1], ring_sum)
        at(LAG[2], ring_end)

        @pl.when(n == NY - 2)
        def _():
            v_copy.wait_recv()
            build(valid2, choose2)

        @pl.when(n < NY)
        def _():
            correlate_own(n)

        @pl.when((n >= NY) & (n < chunks) & ((n - NY) % 4 == 0))
        def _():
            unpack((n - NY) // 2)

        @pl.when((n >= NY) & (n < chunks))
        def _():
            correlate_both(n - NY)

        @pl.when(n < chunks)
        def _():
            for i in range(4):
                ring(n)(i).start()

        return 0

    lax.fori_loop(0, chunks + max(LAG), slot, 0)

    loop(nb, lambda e: rs_copy(e).wait_send(), b)
    loop(nr, lambda r: ag_copy(r).wait_send(), part)
    loop(nr, lambda r: fw_copy(r).wait_send())

    v_copy.wait_send()

    def drain_piece(i):
        pk_copy(i).wait_send()
        sb_copy(i).wait_send()

    loop(PIECES, drain_piece)

    def drain(n):
        z2(n).wait_send()
        for i in range(6):
            ring(n)(i).wait_send()

    loop(chunks, drain)


def on_device(traces, valid, panel_owner, panel_start):
    channels, windows_here, segments, length = traces.shape
    m_count = windows_here * segments
    nb = lax.axis_size("block")
    nt = lax.axis_size("tm")
    nr = nb // 2
    ny = nt // 2
    lanes = length // nr
    forward = jnp.asarray(forward_t(length))
    inverse = jnp.asarray(
        inverse_rows(length, 1.0 / math.sqrt(length // 2 * m_count * nt))
    )
    bf16, f32 = jnp.bfloat16, jnp.float32
    dma = pltpu.SemaphoreType.DMA
    vmem = pl.BlockSpec(memory_space=pltpu.VMEM)
    hbm = pl.BlockSpec(memory_space=pl.ANY)
    smem = pl.BlockSpec(memory_space=pltpu.SMEM)
    chunks = NY + 2 * NW
    work = NY + NW
    unit = (RJ, channels)
    cross = pl.pallas_call(
        functools.partial(kernel, (nb, nt, segments, length)),
        out_shape=jax.ShapeDtypeStruct((2, chunks) + unit, bf16),
        in_specs=[hbm, hbm, vmem, smem, smem],
        out_specs=vmem,
        scratch_shapes=[
            pltpu.VMEM((channels, segments, windows_here, length), bf16),
            pltpu.VMEM((length, length), bf16),
            pltpu.VMEM((m_count, length, channels), f32),
            pltpu.VMEM((m_count, 1, channels), f32),
            pltpu.VMEM((work, ny, 2, 2) + unit, bf16),
            pltpu.VMEM((length, 256), f32),
            pltpu.VMEM((nr, 2, 32, lanes), bf16),
            pltpu.VMEM((nr, 2, m_count * 2 * NP, lanes), bf16),
            pltpu.VMEM((nb, 32, lanes), bf16),
            pltpu.VMEM((segments, windows_here, channels), jnp.int32),
            pltpu.VMEM((m_count, 1, channels), f32),
            pltpu.VMEM((CAP // 256, 256, m_count * channels), bf16),
            pltpu.VMEM((CAP // 256, 256, m_count * channels), bf16),
            pltpu.VMEM(((PIECES - 2) * 2 * PB, m_count * channels), bf16),
            pltpu.VMEM((PIECES, 2 * PB, CAP), bf16),
            pltpu.VMEM((PIECES, 2 * PB, CAP), bf16),
            pltpu.VMEM((m_count, 4 * PB, channels), f32),
            pltpu.VMEM((PIECES, 2, PB, 256), bf16),
            pltpu.VMEM((PIECES, 2, PB, 256), bf16),
            pltpu.VMEM((NY, 2) + unit, f32),
            pltpu.VMEM((work, 2) + unit, bf16),
            pltpu.VMEM((work, 2) + unit, bf16),
            pltpu.VMEM((work, 2, 2) + unit, bf16),
            pltpu.VMEM((work, 2, 2) + unit, bf16),
            pltpu.VMEM((work, 2) + unit, bf16),
            pltpu.VMEM((work, 2) + unit, bf16),
            dma((segments,)), dma, dma((nb,)), dma((nb,)), dma((nr,)), dma((nr,)), dma((nr, 2)),
            dma, dma, dma((PIECES,)), dma((PIECES,)), dma((PIECES,)), dma((PIECES,)),
            dma((work, 6)), dma((work,)), dma((work,)), dma((work, 2)), dma((work, 2)),
            dma((work,)), dma((work,)),
        ],
        compiler_params=pltpu.CompilerParams(
            collective_id=0, has_side_effects=True, vmem_limit_bytes=60 * 2**20
        ),
        name="cross",
    )(traces.transpose(0, 2, 1, 3), forward, valid.transpose(2, 1, 0), panel_owner, panel_start)
    cross = cross.reshape(2, length, channels)
    return lax.dot_general(
        cross, inverse, (((1,), (0,)), ((), ())), preferred_element_type=f32
    )


def solution(mesh):
    in_specs = (P("block", "tm", None, None), P("block", "tm", None), P(), P())
    out_specs = P("tm", "block", None)
    return jax.shard_map(
        on_device, mesh=mesh, in_specs=in_specs, out_specs=out_specs, check_vma=False
    )
```

```python
import functools
import math

import jax
import jax.numpy as jnp
import ml_dtypes
import numpy as np
from jax import lax
from jax.experimental import pallas as pl
from jax.experimental.pallas import tpu as pltpu
from jax.sharding import PartitionSpec as P

MESH = pl.DeviceIdType.MESH
PP = 4
NP = 4
J = PP * NP
GB = 8
PAIR = 2 * GB
KB = PAIR
RJ = 2 * PAIR
NY = 8
NW = 12
PB = 2 * KB
PIECES = NW * KB // PB
CAP = 1536
LAG = (3, 6, 17)
NT = (((1,), (1,)), ((), ()))


def forward_t(length):
    k = np.arange(length // 2)
    n = np.arange(length)
    a = (k[:, None] * n[None, :] % length) * (2.0 * math.pi / length)
    return np.concatenate([np.cos(a), -np.sin(a)], axis=0).astype(np.float32).astype(ml_dtypes.bfloat16)


def inverse_rows(length, factor):
    bins = length // 2
    k = np.arange(bins)
    t = np.arange(length)
    a = (k[:, None] * t[None, :] % length) * (2.0 * math.pi / length)
    w = np.where(k == 0, 1.0, 2.0)[:, None] * factor
    full = np.stack([w * np.cos(a), -w * np.sin(a)])
    full = full.reshape(2, bins // PAIR, PAIR, length).transpose(1, 0, 2, 3)
    return full.reshape(length, length).astype(np.float32).astype(ml_dtypes.bfloat16)


def kernel(dims, x_hbm, ft_hbm, valid, owner, first, c_out, xv, ftv, w, scale, p, s, slab, xs,
           rsb, valid2, pos, choose, choose2, pick, packed, packed2, w2, sb, sb2,
           keep, yfl, yfr, yrl, yrr, zs, rz2,
           x_sem, ft_sem, rs_send, rs_recv, ag_send, fw_send, ag_recv,
           v_send, v_recv, pk_send, pk_recv, sb_send, sb_recv,
           yy_send, yfl_recv, yfr_recv, yrl_recv, yrr_recv, z2_send, z2_recv):
    nb, nt, segments, length = dims
    m_count = 2 * segments
    bins = length // 2
    channels = c_out.shape[-1]
    ny = nt // 2
    nr = nb // 2
    lanes = length // nr
    b = lax.axis_index("block")
    t = lax.axis_index("tm")
    part = b // 2
    core = b % 2
    y = t // 2
    z = t % 2
    right = (b, (y + 1) % ny * 2 + z)
    left = (b, (y + ny - 1) % ny * 2 + z)
    across = (b, y * 2 + 1 - z)
    sibling = (part * 2 + 1 - core, t)
    yr = (y + 1) % ny
    yl = (y + ny - 1) % ny
    yo = (y + 2) % ny

    def remote(src, dst, send, recv, device):
        return pltpu.make_async_remote_copy(
            src_ref=src, dst_ref=dst, send_sem=send, recv_sem=recv,
            device_id=device, device_id_type=MESH,
        )

    def iota(shape, axis):
        return lax.broadcasted_iota(jnp.int32, shape, axis)

    def loop(count, body, skip=None):
        def step(i, _):
            if skip is None:
                body(i)
            else:
                pl.when(i != skip)(lambda: body(i))
            return 0

        lax.fori_loop(0, count, step, 0)

    def load(g):
        return pltpu.make_async_copy(x_hbm.at[:, g], xv.at[:, g], x_sem.at[g])

    loop(segments, lambda g: load(g).start())
    pltpu.make_async_copy(ft_hbm, ftv, ft_sem).start()

    barrier = pltpu.get_barrier_semaphore()

    def greet(device):
        pl.semaphore_signal(barrier, inc=1, device_id=device, device_id_type=MESH)

    loop(nb, lambda e: greet((e, t)), b)
    for device in (right, left, across):
        greet(device)

    places = CAP // channels

    def lane_block(m):
        start = m * channels
        return pl.ds(start if isinstance(m, int) else pl.multiple_of(start, channels), channels)

    def by_segment(body):
        for m in range(places - 1):
            body(m, m + 1)

        def step(m, _):
            body(m, places)
            return 0

        lax.fori_loop(places - 1, m_count, step, 0)

    def build(valid_ref, choose_ref):
        good = valid_ref[...].reshape(m_count, channels).astype(jnp.float32)
        good = jnp.concatenate([good, jnp.zeros((16 - m_count, channels), jnp.float32)], axis=0)
        narrow = good.astype(jnp.bfloat16)
        before = (iota((channels, channels), 0) < iota((channels, channels), 1))
        before = before.astype(jnp.float32).astype(jnp.bfloat16)
        rank = jnp.dot(narrow, before, preferred_element_type=jnp.float32)
        above = (iota((16, 16), 1) < iota((16, 16), 0)).astype(jnp.float32).astype(jnp.bfloat16)
        rank = rank + jnp.sum(
            jnp.dot(above, narrow, preferred_element_type=jnp.float32), axis=1, keepdims=True
        )
        rank = jnp.where(good > 0.0, rank, -1.0)
        for m in range(m_count):
            pos[m] = rank[m:m + 1]

        number = iota((256, channels), 0).astype(jnp.float32)

        def fill(m, count):
            for c in range(count):
                hit = jnp.where(number + 256.0 * c == pos[m], 1.0, 0.0).astype(jnp.bfloat16)
                choose_ref[c, :, lane_block(m)] = hit

        by_segment(fill)

    build(valid, choose)

    loop(segments, lambda g: load(g).wait())
    start = 0
    for panel in range(NP):
        start = start + jnp.where(owner[panel] == b, first[panel], 0)
    valid_rows = valid[...].reshape(m_count, channels).astype(jnp.float32)
    for q in range(PP):
        good = jnp.sum(
            jnp.where(iota((m_count, channels), 1) == start + q, valid_rows, 0.0),
            axis=1, keepdims=True,
        )
        rows = xv[start + q].reshape(m_count, length).astype(jnp.float32) * good
        rows = jnp.concatenate([rows, jnp.zeros((16 - m_count, length), jnp.float32)], axis=0)
        rows = rows.astype(jnp.bfloat16)
        for r in range(nr):
            slab[r, q // 2, pl.ds(q % 2 * 16, 16), :] = rows[:, r * lanes:(r + 1) * lanes]
    pl.semaphore_wait(barrier, nb - 1 + 3)

    def rs_copy(e):
        return remote(slab.at[e // 2, e % 2], rsb.at[b], rs_send.at[e], rs_recv.at[b], (e, t))

    def rs_arrived(e):
        remote(slab.at[part, core], rsb.at[e], rs_send.at[e], rs_recv.at[e], (e, t)).wait_recv()

    loop(nb, lambda e: rs_copy(e).start(), b)
    v_copy = remote(valid, valid2, v_send, v_recv, across)
    v_copy.start()

    order = iota((256, 256), 1) == iota((256, 256), 0) % 128 * 2 + iota((256, 256), 0) // 128
    order = order.astype(jnp.float32).astype(jnp.bfloat16)

    def transform(g):
        halves = []
        for h in range(2):
            mixed = xv[pl.ds(h * 128, 128), g].reshape(256, length)
            halves.append(
                jnp.dot(order, mixed, preferred_element_type=jnp.float32).astype(jnp.bfloat16)
            )
        for v in range(2):
            m = g * 2 + v
            rows = jnp.concatenate([half[v * 128:(v + 1) * 128] for half in halves], axis=0)
            spectrum = lax.dot_general(ftv[...], rows, NT, preferred_element_type=jnp.float32)
            w[m] = spectrum
            energy = jnp.sum(spectrum * spectrum, axis=0, keepdims=True) * (1.0 / length)
            scale[m] = lax.rsqrt(energy + 1e-06) * valid[g, pl.ds(v, 1), :].astype(jnp.float32)

    def transforms(low, high):
        def step(g, _):
            transform(g)
            return 0

        lax.fori_loop(low, high, step, 0)

    pltpu.make_async_copy(ft_hbm, ftv, ft_sem).wait()
    transforms(0, 3)

    rsb[b] = slab[part, core]
    loop(nb, rs_arrived, b)
    shape = (m_count * 2 * NP, nb * 32)
    row, lane = iota(shape, 0), iota(shape, 1)
    wanted = jnp.zeros(shape, jnp.int32)
    for panel in range(NP):
        wanted = jnp.where(row // 2 % NP == panel, owner[panel], wanted)
    choice = (
        (lane // 32 == wanted) & (lane // 16 % 2 == row % 2) & (lane % 16 == row // (2 * NP))
    )
    picked = jnp.dot(
        choice.astype(jnp.float32).astype(jnp.bfloat16), rsb[...].reshape(nb * 32, lanes),
        preferred_element_type=jnp.float32,
    )
    xs[part, core] = picked.astype(jnp.bfloat16)

    def ag_copy(r):
        return remote(xs.at[part, core], xs.at[part, core], ag_send.at[r],
                      ag_recv.at[part, core], (2 * r + core, t))

    def fw_copy(r):
        return remote(xs.at[r, core], xs.at[r, core], fw_send.at[r], ag_recv.at[r, core], sibling)

    def arrived(r, h):
        remote(xs.at[r, h], xs.at[r, h], fw_send.at[r], ag_recv.at[r, h], sibling).wait_recv()

    loop(nr, lambda r: ag_copy(r).start(), part)
    fw_copy(part).start()
    transforms(3, segments)

    def forward(r):
        arrived(r, core)
        fw_copy(r).start()

    loop(nr, forward, part)

    def w_bin(half, i):
        return NY * KB + half * (NW * KB) + i * PB

    def pack(i, count):
        for m in range(m_count):
            rows = []
            for piece in range(count):
                for base in (0, bins):
                    k0 = pl.multiple_of(base + w_bin(1 - z, i + piece), PB)
                    rows.append(w[m, pl.ds(k0, PB), :] * scale[m])
            pick[0:count * 2 * PB, m * channels:(m + 1) * channels] = (
                jnp.concatenate(rows, axis=0).astype(jnp.bfloat16)
            )

        for c in range(places):
            part_c = lax.dot_general(
                pick[0:count * 2 * PB, c * channels:], choose[c, :, c * channels:], NT,
                preferred_element_type=jnp.float32,
            )
            part_c = part_c.astype(jnp.bfloat16).reshape(count, 2 * PB, 256)
            packed[i:i + count, :, c * 256:(c + 1) * 256] = part_c

    def pk_copy(i):
        return remote(packed.at[i], packed2.at[i], pk_send.at[i], pk_recv.at[i], across)

    def sb_copy(i):
        return remote(sb.at[i], sb2.at[i], sb_send.at[i], sb_recv.at[i], across)

    pack(0, 2)
    pk_copy(0).start()
    pk_copy(1).start()
    loop(nr, lambda r: arrived(r, 1 - core))

    half_rows = []
    for h in range(2):
        half_rows.append(jnp.concatenate([xs[r, h] for r in range(nr)], axis=1))
        half_rows.append(jnp.zeros((128 - m_count * 2 * NP, length), jnp.bfloat16))
    source_rows = jnp.concatenate(half_rows, axis=0)
    spectrum = lax.dot_general(ftv[...], source_rows, NT, preferred_element_type=jnp.float32)
    energy = jnp.sum(spectrum * spectrum, axis=0, keepdims=True) * (1.0 / length)
    s[...] = spectrum * lax.rsqrt(energy + 1e-06)

    def narrow_sources(i):
        for o, base in enumerate((0, bins)):
            k0 = pl.multiple_of(base + w_bin(1 - z, i), PB)
            sb[i, o] = s[pl.ds(k0, PB), :].astype(jnp.bfloat16)

    loop(PIECES, narrow_sources)
    sb_copy(0).start()
    sb_copy(1).start()


    def source_matrix(real_tile, imag_tile):
        row, lane = iota((128, 256), 0), iota((128, 256), 1)
        channel = lane // 2 % NP * PP + lane // 128 * 2 + lane % 2
        copies = (row // GB == channel).astype(jnp.float32).astype(jnp.bfloat16)
        segment = row // GB == lane // (2 * NP) % 16
        diagonal = row % GB == lane % GB
        stacked = jnp.concatenate(
            [jnp.where(segment, jnp.concatenate([tile] * 16, axis=0), 0.0)
             for tile in (real_tile, imag_tile)], axis=0,
        ).astype(jnp.bfloat16)
        real = lax.dot_general(copies, stacked, NT, preferred_element_type=jnp.float32)
        real = jnp.where(diagonal, real, 0.0)
        imag = jnp.concatenate([-real[:, 128:], real[:, :128]], axis=1)
        return jnp.concatenate([real, imag], axis=0).astype(jnp.bfloat16)

    def channel_matrix(tile):
        rows = []
        for o in range(2):
            rows += [tile(o, m) for m in range(m_count)]
            rows.append(jnp.zeros((128 - m_count * GB, channels), jnp.float32))
        return jnp.concatenate(rows, axis=0).astype(jnp.bfloat16)

    def own_tile(k0):
        def tile(o, m):
            return w[m, pl.ds(pl.multiple_of(o * bins + k0, GB), GB), :] * scale[m]

        return tile

    def own_source(o, k0):
        return s[pl.ds(pl.multiple_of(o * bins + k0, GB), GB), :]

    def store_chunk(n, groups):
        groups = [g.reshape(2, J, GB, channels) for g in groups]
        both = jnp.concatenate(groups, axis=2).astype(jnp.bfloat16)
        both = both.reshape(2, ny, 2, 2, PAIR, channels)
        for o in range(2):
            p[n, :, :, :, pl.ds(o * PAIR, PAIR), :] = both[o]

    def correlate_own(n):
        groups = []
        for g in range(2):
            k0 = n * KB + g * GB
            groups.append(jnp.dot(
                source_matrix(own_source(0, k0), own_source(1, k0)),
                channel_matrix(own_tile(k0)), preferred_element_type=jnp.float32,
            ))
        store_chunk(n, groups)

    def correlate_both(k):
        i, half = k // 2, k % 2
        far = [sb2[i, o, pl.ds(pl.multiple_of(half * PAIR, PAIR), PAIR), :].astype(jnp.float32)
               for o in range(2)]
        groups = []
        for g in range(2):
            k0 = w_bin(z, 0) + k * KB + g * GB
            near = source_matrix(own_source(0, k0), own_source(1, k0))
            other = source_matrix(*[f[g * GB:(g + 1) * GB] for f in far])

            def far_tile(o, m):
                row = (i % 2 * 2 + o) * PB + half * PAIR + g * GB
                return w2[m, pl.ds(pl.multiple_of(row, GB), GB), :]

            groups.append(jnp.dot(
                jnp.concatenate([near, other], axis=1),
                jnp.concatenate(
                    [channel_matrix(own_tile(k0)), channel_matrix(far_tile)], axis=0
                ),
                preferred_element_type=jnp.float32,
            ))
        store_chunk(NY + k, groups)

    def unpack(i):
        for piece in range(2):
            pk_copy(i + piece).wait_recv()
            sb_copy(i + piece).wait_recv()
        rows = packed2[pl.ds(i, 2)].reshape(4 * PB, CAP)

        def body(m, count):
            lanes_m = lane_block(m)
            side = choose2[0:count, :, lanes_m].reshape(count * channels, channels)
            w2[m] = jnp.dot(
                rows[:, :count * channels], side, preferred_element_type=jnp.float32
            )

        by_segment(body)

    def ring(n):
        def copy(i):
            src, dst, recv, device = (
                lambda: (p.at[n, yo, 0], yfl.at[n], yfl_recv.at[n], right),
                lambda: (p.at[n, yo, 1], yfr.at[n], yfr_recv.at[n], left),
                lambda: (p.at[n, yr, 1], yrl.at[n, 1], yrl_recv.at[n, 1], right),
                lambda: (p.at[n, yl, 0], yrr.at[n, 0], yrr_recv.at[n, 0], left),
                lambda: (yfl.at[n], yrl.at[n, 0], yrl_recv.at[n, 0], right),
                lambda: (yfr.at[n], yrr.at[n, 1], yrr_recv.at[n, 1], left),
            )[i]()
            return remote(src, dst, yy_send.at[n, i], recv, device)

        return copy

    def add(a, c):
        return (a.astype(jnp.float32) + c.astype(jnp.float32)).astype(jnp.bfloat16)

    def z2(n):
        return remote(zs.at[n], rz2.at[n], z2_send.at[n], z2_recv.at[n], across)

    def ring_pass(n):
        copies = ring(n)
        copies(0).wait_recv()
        yfl[n] = add(yfl[n], p[n, yr, 0])
        copies(4).start()
        copies(1).wait_recv()
        yfr[n] = add(yfr[n], p[n, yl, 1])
        copies(5).start()

    def ring_sum(n):
        copies = ring(n)
        for i in (2, 3, 4, 5):
            copies(i).wait_recv()
        total = (p[n, y].astype(jnp.float32) + yrl[n].astype(jnp.float32)
                 + yrr[n].astype(jnp.float32))
        zs[n] = jnp.where(z == 0, total[1], total[0]).astype(jnp.bfloat16)
        z2(n).start()
        mine = jnp.where(z == 0, total[0], total[1])

        @pl.when(n < NY)
        def _():
            keep[n] = mine

        @pl.when(n >= NY)
        def _():
            c_out[:, n + z * NW] = mine.astype(jnp.bfloat16)

    def ring_end(n):
        z2(n).wait_recv()

        @pl.when(n < NY)
        def _():
            c_out[:, n] = (keep[n] + rz2[n].astype(jnp.float32)).astype(jnp.bfloat16)

        @pl.when(n >= NY)
        def _():
            c_out[:, n + (1 - z) * NW] = rz2[n]

    chunks = NY + NW

    def slot(n, _):
        def at(lag, body):
            pl.when((n >= lag) & (n < chunks + lag))(lambda: body(n - lag))

        @pl.when(n == NY // 2)
        def _():
            pack(2, PIECES - 2)
            for i in range(2, PIECES):
                pk_copy(i).start()
                sb_copy(i).start()

        at(LAG[0], ring_pass)
        at(LAG[1], ring_sum)
        at(LAG[2], ring_end)

        @pl.when(n == NY - 2)
        def _():
            v_copy.wait_recv()
            build(valid2, choose2)

        @pl.when(n < NY)
        def _():
            correlate_own(n)

        @pl.when((n >= NY) & (n < chunks) & ((n - NY) % 4 == 0))
        def _():
            unpack((n - NY) // 2)

        @pl.when((n >= NY) & (n < chunks))
        def _():
            correlate_both(n - NY)

        @pl.when(n < chunks)
        def _():
            for i in range(4):
                ring(n)(i).start()

        return 0

    lax.fori_loop(0, chunks + max(LAG), slot, 0)

    loop(nb, lambda e: rs_copy(e).wait_send(), b)
    loop(nr, lambda r: ag_copy(r).wait_send(), part)
    loop(nr, lambda r: fw_copy(r).wait_send())

    v_copy.wait_send()

    def drain_piece(i):
        pk_copy(i).wait_send()
        sb_copy(i).wait_send()

    loop(PIECES, drain_piece)

    def drain(n):
        z2(n).wait_send()
        for i in range(6):
            ring(n)(i).wait_send()

    loop(chunks, drain)


def on_device(traces, valid, panel_owner, panel_start):
    channels, windows_here, segments, length = traces.shape
    m_count = windows_here * segments
    nb = lax.axis_size("block")
    nt = lax.axis_size("tm")
    nr = nb // 2
    ny = nt // 2
    lanes = length // nr
    forward = jnp.asarray(forward_t(length))
    inverse = jnp.asarray(
        inverse_rows(length, 1.0 / math.sqrt(length // 2 * m_count * nt))
    )
    bf16, f32 = jnp.bfloat16, jnp.float32
    dma = pltpu.SemaphoreType.DMA
    vmem = pl.BlockSpec(memory_space=pltpu.VMEM)
    hbm = pl.BlockSpec(memory_space=pl.ANY)
    smem = pl.BlockSpec(memory_space=pltpu.SMEM)
    chunks = NY + 2 * NW
    work = NY + NW
    unit = (RJ, channels)
    cross = pl.pallas_call(
        functools.partial(kernel, (nb, nt, segments, length)),
        out_shape=jax.ShapeDtypeStruct((2, chunks) + unit, bf16),
        in_specs=[hbm, hbm, vmem, smem, smem],
        out_specs=vmem,
        scratch_shapes=[
            pltpu.VMEM((channels, segments, windows_here, length), bf16),
            pltpu.VMEM((length, length), bf16),
            pltpu.VMEM((m_count, length, channels), f32),
            pltpu.VMEM((m_count, 1, channels), f32),
            pltpu.VMEM((work, ny, 2, 2) + unit, bf16),
            pltpu.VMEM((length, 256), f32),
            pltpu.VMEM((nr, 2, 32, lanes), bf16),
            pltpu.VMEM((nr, 2, m_count * 2 * NP, lanes), bf16),
            pltpu.VMEM((nb, 32, lanes), bf16),
            pltpu.VMEM((segments, windows_here, channels), jnp.int32),
            pltpu.VMEM((m_count, 1, channels), f32),
            pltpu.VMEM((CAP // 256, 256, m_count * channels), bf16),
            pltpu.VMEM((CAP // 256, 256, m_count * channels), bf16),
            pltpu.VMEM(((PIECES - 2) * 2 * PB, m_count * channels), bf16),
            pltpu.VMEM((PIECES, 2 * PB, CAP), bf16),
            pltpu.VMEM((PIECES, 2 * PB, CAP), bf16),
            pltpu.VMEM((m_count, 4 * PB, channels), f32),
            pltpu.VMEM((PIECES, 2, PB, 256), bf16),
            pltpu.VMEM((PIECES, 2, PB, 256), bf16),
            pltpu.VMEM((NY, 2) + unit, f32),
            pltpu.VMEM((work, 2) + unit, bf16),
            pltpu.VMEM((work, 2) + unit, bf16),
            pltpu.VMEM((work, 2, 2) + unit, bf16),
            pltpu.VMEM((work, 2, 2) + unit, bf16),
            pltpu.VMEM((work, 2) + unit, bf16),
            pltpu.VMEM((work, 2) + unit, bf16),
            dma((segments,)), dma, dma((nb,)), dma((nb,)), dma((nr,)), dma((nr,)), dma((nr, 2)),
            dma, dma, dma((PIECES,)), dma((PIECES,)), dma((PIECES,)), dma((PIECES,)),
            dma((work, 6)), dma((work,)), dma((work,)), dma((work, 2)), dma((work, 2)),
            dma((work,)), dma((work,)),
        ],
        compiler_params=pltpu.CompilerParams(
            collective_id=0, has_side_effects=True, vmem_limit_bytes=60 * 2**20
        ),
        name="cross",
    )(traces.transpose(0, 2, 1, 3), forward, valid.transpose(2, 1, 0), panel_owner, panel_start)
    cross = cross.reshape(2, length, channels)
    return lax.dot_general(
        cross, inverse, (((1,), (0,)), ((), ())), preferred_element_type=f32
    )


def solution(mesh):
    in_specs = (P("block", "tm", None, None), P("block", "tm", None), P(), P())
    out_specs = P("tm", "block", None)
    return jax.shard_map(
        on_device, mesh=mesh, in_specs=in_specs, out_specs=out_specs, check_vma=False
    )
```
